32 devices in a mesh: groups: 2 (over y), dp: 4 (over x, core), tensor: 4 (over z).
Axes of the slice: x: 2, y: 2, z: 4, core: 2. Of those that a mesh axis runs over, the one named last changes fastest.
Arguments:
- queries: bfloat16 [640, 16384], P(('groups', 'dp'), 'tensor'), parts along dimension 0, may hold values from -8 to 8, as said below
- kv_pool: bfloat16 [80, 8, 64, 256], P(('groups', 'dp')), parts along dimension 0, may hold values from -8 to 8, as said below
- out_weight: bfloat16 [16384, 16384], P('tensor', 'dp'), may hold values from -0.046875 to 0.046875
- residual: bfloat16 [640, 16384], P(('groups', 'tensor'), 'dp'), parts along dimension 0, may hold values from -1.5 to 1.5
- block_lists: int32 [640, 8], P(('groups', 'dp')), parts along dimension 0, may hold values from 0 to 39, as said below
- lengths: int32 [640], P(('groups', 'dp')), parts along dimension 0, may hold values from 1 to 512, as said below
Outputs:
- mixed: bfloat16 [640, 16384], P(('groups', 'tensor'), 'dp'), parts along dimension 0
The draws below stay inside these ranges and needn't reach their ends.
There are 2 independent parts, one for each index of `groups`. The reference program is written for one: setup_inputs(seed, part) draws one part's arguments, and reference() takes and returns one part's arrays. A program takes and returns all parts, laid end to end along the dimension named above; an argument that names none is the same for every part. Nothing has to cross between parts.
Inputs may be any that keep to these rules, and one draw needn't show every extreme that they name: The values of the queries and of the cached keys and values lie in this range. `kv_pool`: as for queries. `block_lists`: each row names 8 distinct blocks, 2 stored on each index of dp. The rows of one index of dp (aligned blocks of 80 rows) name exactly 4 distinct blocks stored on each index of dp. `lengths`: some row has the full length.
All inputs are finite; a program needn't handle non-finite values.
Results may differ from the reference program's by a relative error of at most 0.01.
Values may be sent and summed in bfloat16 or wider, within the bound.
A program may use at most 192 MiB of HBM per device.

```python
import math
import jax
import jax.numpy as jnp
from jax import lax

D = 16384
HEADS = 128
KVH = 8
HD = 128
BLK = 64
R_DEV = 80
NB_DEV = 10
WIN = 2
CAP = 4
MAXB = 8
ROWS = 320
NBLOCKS = 40
N_DP = 4
N_TENSOR = 4


def draw_queries(key, part):
    key = jax.random.fold_in(key, 3)
    second_key = jax.random.fold_in(key, 1)
    values = jnp.clip(jax.random.normal(second_key, (ROWS, HEADS, HD), jnp.float32), -6.0, 6.0)
    return values.reshape(ROWS, HEADS * HD).astype(jnp.bfloat16)


def draw_kv_pool(key, part):
    key = jax.random.fold_in(key, 11)
    second_key = jax.random.fold_in(key, 1)
    pool_shape = (NBLOCKS, KVH, BLK, 2 * HD)
    values = jnp.clip(jax.random.normal(second_key, pool_shape, jnp.float32), -6.0, 6.0)
    return values.astype(jnp.bfloat16)


def draw_block_lists(key, part):
    key = jax.random.fold_in(key, 5)
    subset_key, shift_key, jitter_key, order_key = jax.random.split(key, 4)
    subset_keys = jax.random.split(subset_key, N_DP * N_DP)
    subsets = jax.vmap(lambda sub_key: jax.random.permutation(sub_key, NB_DEV)[:CAP])(subset_keys)
    subsets = subsets.astype(jnp.int32).reshape(N_DP, N_DP, CAP)
    shifts = jax.random.randint(shift_key, (N_DP, N_DP), 0, CAP)
    row_ids = jnp.arange(ROWS, dtype=jnp.int32)
    device_of = row_ids // R_DEV
    local_row = row_ids % R_DEV
    jitter = jax.random.randint(jitter_key, (ROWS,), 0, CAP) * (local_row >= 2).astype(jnp.int32)
    window = jnp.arange(WIN, dtype=jnp.int32)
    slot_index = (local_row[:, None, None] * WIN + window[None, None, :] + shifts[device_of][:, :, None] + jitter[:, None, None]) % CAP
    slot_values = jnp.take_along_axis(subsets[device_of], slot_index, axis=2)
    owner_ids = jnp.arange(N_DP, dtype=jnp.int32)
    block_ids = (owner_ids[None, :, None] * NB_DEV + slot_values).reshape(ROWS, MAXB)
    order_keys = jax.random.split(order_key, ROWS)
    orders = jax.vmap(lambda row_key: jax.random.permutation(row_key, MAXB))(order_keys)
    return jnp.take_along_axis(block_ids, orders.astype(jnp.int32), axis=1).astype(jnp.int32)


def draw_lengths(key, part):
    key = jax.random.fold_in(key, 7)
    first_key, second_key = jax.random.split(key)
    longest = MAXB * BLK
    drawn = jax.random.randint(first_key, (ROWS,), 1, longest + 1)
    chosen = jax.random.randint(second_key, (), 0, ROWS)
    return jnp.where(jnp.arange(ROWS) == chosen, longest, drawn).astype(jnp.int32)


def steps_of(rng, dims, cuts, low, high):
    factor_of, own = 1.0, jax.random.fold_in(rng, 6)
    for position, shards_of in cuts:
        steps = jnp.exp(jax.random.uniform(jax.random.fold_in(own, position), (shards_of,), jnp.float32, low / len(cuts), high / len(cuts)))
        factor_of = factor_of * jnp.repeat(steps, dims[position] // shards_of).reshape([-1 if axis == position else 1 for axis in range(len(dims))])
    return factor_of


def normal_values(own_key, dims, deviation, limit, cuts=(), kind=jnp.bfloat16):
    factor_of = steps_of(own_key, dims, cuts, -0.22, 0.18) if cuts else 1.0
    array = jax.random.normal(own_key, dims, jnp.float32) * deviation * factor_of
    return jnp.minimum(jnp.maximum(array, -limit), limit).astype(kind)


def setup_inputs(seed: int = 0, part: int = 0) -> dict:
    arg_keys = jax.random.split(jax.random.key(seed), 7)
    own_keys = jax.random.split(jax.random.fold_in(arg_keys[6], part), 7)
    return {
        "queries": draw_queries(jax.random.fold_in(jax.random.fold_in(arg_keys[6], part), 71), part),
        "kv_pool": draw_kv_pool(jax.random.fold_in(jax.random.fold_in(arg_keys[6], part), 71), part),
        "out_weight": normal_values(arg_keys[2], (HEADS * HD, D), (HEADS * HD) ** -0.5, 0.046875, ((0, 4), (1, 4))),
        "residual": normal_values(own_keys[3], (ROWS, D), 0.25, 1.5, ((0, 4), (1, 4))),
        "block_lists": draw_block_lists(jax.random.fold_in(jax.random.fold_in(arg_keys[6], part), 71), part),
        "lengths": draw_lengths(jax.random.fold_in(jax.random.fold_in(arg_keys[6], part), 71), part),
    }


def reference(queries, kv_pool, out_weight, residual, block_lists, lengths):
    head_group = HEADS // KVH
    token_count = MAXB * BLK

    def one_row(inputs):
        query_row, named_ids, length_row = inputs
        blocks = kv_pool[named_ids]
        blocks = jnp.transpose(blocks, (1, 0, 2, 3)).reshape(KVH, token_count, 2 * HD)
        key_rows = blocks[:, :, :HD].astype(jnp.float32)
        value_rows = blocks[:, :, HD:].astype(jnp.float32)
        query_heads = query_row.reshape(KVH, head_group, HD).astype(jnp.float32)
        scores = jnp.einsum('kqd,ktd->kqt', query_heads, key_rows, precision=lax.Precision.HIGHEST) / math.sqrt(HD)
        visible = (jnp.arange(token_count) < length_row)[None, None, :]
        row_max = lax.optimization_barrier(jnp.max(jnp.where(visible, scores, -1e+30), axis=2))
        weights = jnp.where(visible, jnp.exp(scores - row_max[:, :, None]), 0.0)
        row_total = lax.optimization_barrier(jnp.sum(weights, axis=2))
        rounded = lax.optimization_barrier(weights.astype(jnp.bfloat16)).astype(jnp.float32)
        summed = jnp.einsum('kqt,ktd->kqd', rounded, value_rows, precision=lax.Precision.HIGHEST)
        return (summed / row_total[:, :, None]).reshape(HEADS * HD).astype(jnp.bfloat16)
    attended = lax.map(one_row, (queries, block_lists, lengths))
    head_width = HEADS * HD // N_TENSOR
    pieces = jnp.transpose(attended.reshape(ROWS, N_TENSOR, head_width), (1, 0, 2))
    weight_pieces = out_weight.reshape(N_TENSOR, head_width, D)

    def add_piece(running, inputs):
        part_in, weight_in = inputs
        partial_value = jnp.dot(part_in, weight_in, preferred_element_type=jnp.float32)
        partial_value = lax.optimization_barrier(partial_value.astype(jnp.bfloat16)).astype(jnp.float32)
        return (running + partial_value, None)
    summed, _ = lax.scan(add_piece, jnp.zeros((ROWS, D), jnp.float32), (pieces, weight_pieces))
    return (residual.astype(jnp.float32) + summed).astype(jnp.bfloat16)
```

```python
import math

import jax
import jax.numpy as jnp
from jax import lax
from jax.experimental import pallas as pl
from jax.experimental.pallas import tpu as pltpu
from jax.sharding import PartitionSpec as P


def attend_blocks(state_in, query_heads, block_ids, block_data, block_lists, lengths, head_dim):
    row_max, row_total, accumulated = state_in
    block_len = block_data.shape[2]
    list_len = block_lists.shape[1]
    matches = block_lists[:, :, None] == block_ids[None, None, :]
    named_any = jnp.any(matches, axis=1)
    position = jnp.sum(
        matches.astype(jnp.int32) * jnp.arange(list_len, dtype=jnp.int32)[None, :, None], axis=1
    )
    offsets = (
        position[:, :, None] * block_len + jnp.arange(block_len, dtype=jnp.int32)[None, None, :]
    )
    visible = named_any[:, :, None] & (offsets < lengths[:, None, None])
    key_part = block_data[..., :head_dim]
    value_part = block_data[..., head_dim:]
    scores = jnp.einsum(
        "rkqd,nkbd->rkqnb", query_heads, key_part, preferred_element_type=jnp.float32
    ) / math.sqrt(head_dim)
    visible_full = visible[:, None, None, :, :]
    piece_max = jnp.max(jnp.where(visible_full, scores, -1e30), axis=(3, 4))
    new_max = jnp.maximum(row_max, piece_max)
    weights = jnp.where(visible_full, jnp.exp(scores - new_max[..., None, None]), 0.0)
    row_total = jnp.sum(weights, axis=(3, 4))
    accumulated = jnp.einsum(
        "rkqnb,nkbd->rkqd",
        weights.astype(jnp.bfloat16),
        value_part,
        preferred_element_type=jnp.float32,
    )
    return (new_max, row_total, accumulated)


def generic_device(queries, kv_pool, out_weight, residual, block_lists, lengths):
    tensor_size = lax.axis_size("tensor")
    row_count, query_width = queries.shape
    store_count, kv_heads, block_len, pair_width = kv_pool.shape
    head_dim = pair_width // 2
    local_heads = query_width // head_dim
    head_group = local_heads * tensor_size // kv_heads
    local_kv = max(1, local_heads // head_group)
    first_kv = lax.axis_index("tensor") * local_heads // head_group
    own_pool = lax.dynamic_slice_in_dim(kv_pool, first_kv, local_kv, 1)
    query_heads = queries.reshape(row_count, local_kv, local_heads // local_kv, head_dim)
    state_shape = (row_count, local_kv, local_heads // local_kv)
    start_state = (
        jnp.full(state_shape, -1e30, jnp.float32),
        jnp.zeros(state_shape, jnp.float32),
        jnp.zeros(state_shape + (head_dim,), jnp.float32),
    )
    shard_blocks = lax.all_gather(own_pool, "dp", axis=0, tiled=True)
    block_ids = jnp.arange(shard_blocks.shape[0], dtype=jnp.int32)
    final_state = attend_blocks(
        start_state, query_heads, block_ids, shard_blocks, block_lists, lengths, head_dim
    )
    row_max, row_total, accumulated = final_state
    attended = (
        (accumulated / row_total[..., None]).astype(jnp.bfloat16).reshape(row_count, query_width)
    )
    partial_value = jnp.dot(
        lax.all_gather(attended, "dp", axis=0, tiled=True),
        out_weight,
        preferred_element_type=jnp.float32,
    )
    summed = lax.psum_scatter(
        partial_value.astype(jnp.bfloat16), "tensor", scatter_dimension=0, tiled=True
    ).astype(jnp.float32)
    return (residual.astype(jnp.float32) + summed).astype(jnp.bfloat16)


MESH = pl.DeviceIdType.MESH
CAP = 4
CHUNK = 512


def fused_kernel(
    q_ref, kv_ref, w_ref, res_ref, bl_ref, len_ref, out_ref,
    w_v, kvb, kc, vc, bias, ids_v, ids_s, attb, stg, rl, rr, facc,
    w_sem, ids_sem, kvl_sem, kv_send, kv_recv, at_send, at_recv, z_send, zl_recv, zr_recv,
):
    rows, width = q_ref.shape
    stores, kv_heads, blk, pair = kv_ref.shape
    hd = pair // 2
    n_dp, nz = attb.shape[0], stg.shape[0]
    slots = CAP * n_dp
    local_heads = width // hd
    local_kv = len(kvb) // 2
    head_group = local_heads // local_kv
    per = CHUNK // hd
    groups_per_kv = head_group // per
    n_att = width // CHUNK
    n_col = w_v.shape[0]
    d = lax.axis_index("dp")
    z = lax.axis_index("tensor")
    x, c = d // 2, d % 2
    mate = 2 * x + (1 - c)
    across = 2 * (1 - x) + c
    diag = 2 * (1 - x) + (1 - c)

    def w_copy(j):
        cols = pl.ds(pl.multiple_of(j * CHUNK, CHUNK), CHUNK)
        return pltpu.make_async_copy(w_ref.at[:, cols], w_v.at[j], w_sem.at[j])

    def kv_src(t):
        return kv_ref.at[:, z * local_kv + t // 2, :, pl.ds((t % 2) * hd, hd)]

    def kv_dst(t, owner):
        return kvb[t].at[pl.ds(owner * stores, stores)]

    def kv_local(t):
        return pltpu.make_async_copy(kv_src(t), kv_dst(t, d), kvl_sem.at[t])

    def kv_remote(kind, t):
        owner = across if kind == 2 else d
        src = kv_dst(t, owner) if kind == 2 else kv_src(t)
        return pltpu.make_async_remote_copy(
            src_ref=src, dst_ref=kv_dst(t, owner),
            send_sem=kv_send.at[kind, t], recv_sem=kv_recv.at[kind, t],
            device_id={"dp": across if kind == 1 else mate}, device_id_type=MESH,
        )

    def att_remote(kind, i):
        owner = across if kind == 2 else d
        cols = pl.ds(pl.multiple_of(i * CHUNK, CHUNK), CHUNK)
        ref = attb.at[owner, :, cols]
        return pltpu.make_async_remote_copy(
            src_ref=ref, dst_ref=ref,
            send_sem=at_send.at[kind, i], recv_sem=at_recv.at[kind, i],
            device_id={"dp": across if kind == 1 else mate}, device_id_type=MESH,
        )

    def z_remote(b, j, right):
        cols = pl.ds(pl.multiple_of(j * CHUNK, CHUNK), CHUNK)
        land, sem = (rl, zl_recv) if right else (rr, zr_recv)
        return pltpu.make_async_remote_copy(
            src_ref=stg.at[b, :, cols], dst_ref=land.at[b, :, cols],
            send_sem=z_send.at[b, j], recv_sem=sem.at[b, j],
            device_id={"tensor": z + 1 if right else z - 1}, device_id_type=MESH,
        )

    for t in range(2 * local_kv):
        kv_local(t).start()
    for j in range(n_col):
        w_copy(j).start()

    barrier = pltpu.get_barrier_semaphore()
    pl.semaphore_signal(barrier, inc=1, device_id={"dp": mate}, device_id_type=MESH)
    pl.semaphore_signal(barrier, inc=1, device_id={"dp": across}, device_id_type=MESH)

    @pl.when(z > 0)
    def _():
        pl.semaphore_signal(barrier, inc=1, device_id={"tensor": z - 1}, device_id_type=MESH)

    @pl.when(z < nz - 1)
    def _():
        pl.semaphore_signal(barrier, inc=1, device_id={"tensor": z + 1}, device_id_type=MESH)

    pl.semaphore_wait(
        barrier, 2 + (z > 0).astype(jnp.int32) + (z < nz - 1).astype(jnp.int32)
    )

    for t in range(2 * local_kv):
        kv_remote(1, t).start()
    for t in range(2 * local_kv):
        kv_remote(0, t).start()

    bl = bl_ref[...]
    list_len = bl.shape[1]
    lane = lax.broadcasted_iota(jnp.int32, (rows, 128), 1)
    hit = jnp.zeros((rows, 128), jnp.int32)
    for k in range(list_len):
        hit = jnp.maximum(hit, (bl[:, k : k + 1] == lane).astype(jnp.int32))
    named_l = jnp.max(hit, axis=0, keepdims=True)
    sub2 = lax.broadcasted_iota(jnp.int32, (128, 128), 0)
    lane2 = lax.broadcasted_iota(jnp.int32, (128, 128), 1)
    named_b = jnp.broadcast_to(named_l, (128, 128))
    named_s = jnp.sum(jnp.where(sub2 == lane2, named_b, 0), axis=1, keepdims=True)
    rank = jnp.sum(jnp.where(lane2 < sub2, named_b, 0), axis=1, keepdims=True)
    picked = jnp.where((rank == lane2) & (named_s > 0), sub2, 0)
    ids = jnp.sum(picked, axis=0, keepdims=True)
    ids_v[...] = jnp.broadcast_to(ids, ids_v.shape)
    ids_copy = pltpu.make_async_copy(ids_v, ids_s, ids_sem)
    ids_copy.start()
    ids_copy.wait()

    eye_r = lax.broadcasted_iota(jnp.int32, (rows, rows), 0)
    eye_c = lax.broadcasted_iota(jnp.int32, (rows, rows), 1)
    len_b = jnp.broadcast_to(len_ref[...], (rows, rows))
    length = jnp.sum(jnp.where(eye_r == eye_c, len_b, 0), axis=1, keepdims=True)
    place = lax.broadcasted_iota(jnp.int32, (rows, list_len), 1)
    token = lax.broadcasted_iota(jnp.int32, (rows, 2 * blk), 1)
    for pair_of in range(slots // 2):
        limits = []
        for k in range(2):
            match = bl == ids_s[0, 2 * pair_of + k]
            left = jnp.where(match, length - place * blk, 0)
            limits.append(jnp.max(left, axis=1, keepdims=True))
        limit = jnp.where(token < blk, jnp.minimum(limits[0], blk), limits[1] + blk)
        bias[:, 2 * blk * pair_of : 2 * blk * (pair_of + 1)] = jnp.where(token < limit, 0.0, -1e30)

    scale = 1.0 / math.sqrt(hd)
    for h in range(local_kv):
        for t in (2 * h, 2 * h + 1):
            kv_remote(1, t).wait_recv()
            kv_remote(2, t).start()
        for t in (2 * h, 2 * h + 1):
            kv_local(t).wait()
            kv_remote(0, t).wait_recv()
            kv_remote(2, t).wait_recv()
        for j in range(slots):
            pick = ids_s[0, j]
            kc[blk * j : blk * (j + 1), :] = kvb[2 * h][pick]
            vc[blk * j : blk * (j + 1), :] = kvb[2 * h + 1][pick]

        @pl.loop(0, groups_per_kv)
        def _(g):
            i = h * groups_per_kv + g
            cols = pl.ds(pl.multiple_of(i * CHUNK, CHUNK), CHUNK)
            qs = q_ref[:, cols]
            stacked = jnp.concatenate(
                [qs[:, hd * k : hd * (k + 1)] for k in range(per)], axis=0
            )
            scores = lax.dot_general(
                stacked, kc[...], (((1,), (1,)), ((), ())), preferred_element_type=jnp.float32
            ).reshape(per, rows, slots * blk)
            scores = scores * scale + bias[...][None]
            top = jnp.max(scores, axis=2, keepdims=True)
            weights = jnp.exp(scores - top)
            total = jnp.sum(weights, axis=2, keepdims=True)
            summed = jnp.dot(
                weights.astype(jnp.bfloat16).reshape(per * rows, slots * blk),
                vc[...], preferred_element_type=jnp.float32,
            ).reshape(per, rows, hd)
            attended = (summed / total).astype(jnp.bfloat16)
            attb[d, :, cols] = jnp.concatenate([attended[k] for k in range(per)], axis=1)
            att_remote(1, i).start()
            att_remote(0, i).start()

    @pl.loop(0, n_att)
    def _(i):
        att_remote(0, i).wait_recv()

    inner = (z > 0) & (z < nz - 1)
    half = nz // 2

    def block_of(s, i):
        chip = jnp.where(s < n_col, x, 1 - x)
        return 2 * chip + jnp.where(z < half, 1 - i, i)

    def send_end(s):
        j = s % n_col
        for i in range(2):
            b = block_of(s, i)

            @pl.when((z == 0) & (b > 0))
            def _():
                z_remote(b, j, True).start()

            @pl.when((z == nz - 1) & (b < nz - 1))
            def _():
                z_remote(b, j, False).start()

    def send_inner(s):
        j = s % n_col
        cols = pl.ds(pl.multiple_of(j * CHUNK, CHUNK), CHUNK)

        def pass_on(b, right):
            land = rl if right else rr
            z_remote(b, j, right).wait_recv()
            added = stg[b, :, cols].astype(jnp.float32) + land[b, :, cols].astype(jnp.float32)
            stg[b, :, cols] = added.astype(jnp.bfloat16)
            z_remote(b, j, right).start()

        for i in range(2):
            b = block_of(s, i)

            @pl.when(inner & (b > z))
            def _():
                pass_on(b, True)

            @pl.when(inner & (b < z))
            def _():
                pass_on(b, False)

    @pl.loop(0, 2 * n_col)
    def _(s):
        j = s % n_col
        cols = pl.ds(pl.multiple_of(j * CHUNK, CHUNK), CHUNK)

        @pl.when(s < n_col)
        def _():
            w_copy(j).wait()
            att_remote(1, j).wait_recv()
            att_remote(2, j).start()

        @pl.when(s == n_col)
        def _():
            @pl.loop(0, n_att)
            def _(i):
                att_remote(2, i).wait_recv()

        chip = jnp.where(s < n_col, x, 1 - x)
        part = attb[pl.ds(2 * chip, 2)].reshape(2 * rows, width)
        partial = jnp.dot(part, w_v[j], preferred_element_type=jnp.float32)
        stg[pl.ds(2 * chip, 2), :, cols] = partial.astype(jnp.bfloat16).reshape(2, rows, CHUNK)
        send_end(s)

        @pl.when(s > 0)
        def _():
            send_inner(s - 1)

    send_inner(2 * n_col - 1)

    @pl.loop(0, n_col)
    def _(j):
        cols = pl.ds(pl.multiple_of(j * CHUNK, CHUNK), CHUNK)
        facc[...] = res_ref[:, cols].astype(jnp.float32) + stg[z, :, cols].astype(jnp.float32)

        @pl.when(z > 0)
        def _():
            z_remote(z, j, True).wait_recv()
            facc[...] += rl[z, :, cols].astype(jnp.float32)

        @pl.when(z < nz - 1)
        def _():
            z_remote(z, j, False).wait_recv()
            facc[...] += rr[z, :, cols].astype(jnp.float32)

        out_ref[:, cols] = facc[...].astype(jnp.bfloat16)

    for kind in range(3):
        for t in range(2 * local_kv):
            kv_remote(kind, t).wait_send()

        @pl.loop(0, n_att)
        def _(i):
            att_remote(kind, i).wait_send()

    @pl.loop(0, n_col)
    def _(j):
        for b in range(nz):

            @pl.when(z < b)
            def _():
                z_remote(b, j, True).wait_send()

            @pl.when(z > b)
            def _():
                z_remote(b, j, False).wait_send()


def fused_device(queries, kv_pool, out_weight, residual, block_lists, lengths):
    n_dp, nz = lax.axis_size("dp"), lax.axis_size("tensor")
    rows, width = queries.shape
    stores, kv_heads, blk, pair = kv_pool.shape
    hd = pair // 2
    columns = out_weight.shape[1]
    local_kv = kv_heads // nz
    n_att, n_col = width // CHUNK, columns // CHUNK
    tokens = CAP * n_dp * blk
    bf16, f32 = jnp.bfloat16, jnp.float32
    dma = pltpu.SemaphoreType.DMA
    vmem = pl.BlockSpec(memory_space=pltpu.VMEM)
    hbm = pl.BlockSpec(memory_space=pl.ANY)
    return pl.pallas_call(
        fused_kernel,
        out_shape=jax.ShapeDtypeStruct((rows, columns), bf16),
        in_specs=[vmem, hbm, hbm, vmem, vmem, vmem],
        out_specs=vmem,
        scratch_shapes=[
            pltpu.VMEM((n_col, width, CHUNK), bf16),
            [pltpu.VMEM((n_dp * stores, blk, hd), bf16)] * (2 * local_kv),
            pltpu.VMEM((tokens, hd), bf16),
            pltpu.VMEM((tokens, hd), bf16),
            pltpu.VMEM((rows, tokens), f32),
            pltpu.VMEM((8, 128), jnp.int32),
            pltpu.SMEM((8, 128), jnp.int32),
            pltpu.VMEM((n_dp, rows, width), bf16),
            pltpu.VMEM((nz, rows, columns), bf16),
            pltpu.VMEM((nz, rows, columns), bf16),
            pltpu.VMEM((nz, rows, columns), bf16),
            pltpu.VMEM((rows, CHUNK), f32),
            dma((n_col,)),
            dma,
            dma((2 * local_kv,)),
            dma((3, 2 * local_kv)),
            dma((3, 2 * local_kv)),
            dma((3, n_att)),
            dma((3, n_att)),
            dma((nz, n_col)),
            dma((nz, n_col)),
            dma((nz, n_col)),
        ],
        compiler_params=pltpu.CompilerParams(
            collective_id=0, has_side_effects=True, vmem_limit_bytes=60 * 1024 * 1024
        ),
        cost_estimate=pl.CostEstimate(
            flops=2 * n_dp * rows * width * columns,
            bytes_accessed=2 * width * columns,
            transcendentals=rows * width // hd * tokens,
        ),
    )(queries, kv_pool, out_weight, residual, block_lists, lengths.reshape(1, rows))


def fits_fused(mesh):
    return mesh.shape["dp"] == 4 and mesh.shape["tensor"] == 4


def solution(mesh):
    in_specs = (
        P(("groups", "dp"), "tensor"),
        P(("groups", "dp"), None, None, None),
        P("tensor", "dp"),
        P(("groups", "tensor"), "dp"),
        P(("groups", "dp"), None),
        P(("groups", "dp")),
    )
    out_specs = P(("groups", "tensor"), "dp")
    body = fused_device if fits_fused(mesh) else generic_device
    return jax.shard_map(
        body, mesh=mesh, in_specs=in_specs, out_specs=out_specs, check_vma=False
    )
```

```python
import math

import jax
import jax.numpy as jnp
from jax import lax
from jax.experimental import pallas as pl
from jax.experimental.pallas import tpu as pltpu
from jax.sharding import PartitionSpec as P


def attend_blocks(state_in, query_heads, block_ids, block_data, block_lists, lengths, head_dim):
    row_max, row_total, accumulated = state_in
    block_len = block_data.shape[2]
    list_len = block_lists.shape[1]
    matches = block_lists[:, :, None] == block_ids[None, None, :]
    named_any = jnp.any(matches, axis=1)
    position = jnp.sum(
        matches.astype(jnp.int32) * jnp.arange(list_len, dtype=jnp.int32)[None, :, None], axis=1
    )
    offsets = (
        position[:, :, None] * block_len + jnp.arange(block_len, dtype=jnp.int32)[None, None, :]
    )
    visible = named_any[:, :, None] & (offsets < lengths[:, None, None])
    key_part = block_data[..., :head_dim]
    value_part = block_data[..., head_dim:]
    scores = jnp.einsum(
        "rkqd,nkbd->rkqnb", query_heads, key_part, preferred_element_type=jnp.float32
    ) / math.sqrt(head_dim)
    visible_full = visible[:, None, None, :, :]
    piece_max = jnp.max(jnp.where(visible_full, scores, -1e30), axis=(3, 4))
    new_max = jnp.maximum(row_max, piece_max)
    weights = jnp.where(visible_full, jnp.exp(scores - new_max[..., None, None]), 0.0)
    row_total = jnp.sum(weights, axis=(3, 4))
    accumulated = jnp.einsum(
        "rkqnb,nkbd->rkqd",
        weights.astype(jnp.bfloat16),
        value_part,
        preferred_element_type=jnp.float32,
    )
    return (new_max, row_total, accumulated)


def generic_device(queries, kv_pool, out_weight, residual, block_lists, lengths):
    tensor_size = lax.axis_size("tensor")
    row_count, query_width = queries.shape
    store_count, kv_heads, block_len, pair_width = kv_pool.shape
    head_dim = pair_width // 2
    local_heads = query_width // head_dim
    head_group = local_heads * tensor_size // kv_heads
    local_kv = max(1, local_heads // head_group)
    first_kv = lax.axis_index("tensor") * local_heads // head_group
    own_pool = lax.dynamic_slice_in_dim(kv_pool, first_kv, local_kv, 1)
    query_heads = queries.reshape(row_count, local_kv, local_heads // local_kv, head_dim)
    state_shape = (row_count, local_kv, local_heads // local_kv)
    start_state = (
        jnp.full(state_shape, -1e30, jnp.float32),
        jnp.zeros(state_shape, jnp.float32),
        jnp.zeros(state_shape + (head_dim,), jnp.float32),
    )
    shard_blocks = lax.all_gather(own_pool, "dp", axis=0, tiled=True)
    block_ids = jnp.arange(shard_blocks.shape[0], dtype=jnp.int32)
    final_state = attend_blocks(
        start_state, query_heads, block_ids, shard_blocks, block_lists, lengths, head_dim
    )
    row_max, row_total, accumulated = final_state
    attended = (
        (accumulated / row_total[..., None]).astype(jnp.bfloat16).reshape(row_count, query_width)
    )
    partial_value = jnp.dot(
        lax.all_gather(attended, "dp", axis=0, tiled=True),
        out_weight,
        preferred_element_type=jnp.float32,
    )
    summed = lax.psum_scatter(
        partial_value.astype(jnp.bfloat16), "tensor", scatter_dimension=0, tiled=True
    ).astype(jnp.float32)
    return (residual.astype(jnp.float32) + summed).astype(jnp.bfloat16)


MESH = pl.DeviceIdType.MESH
CAP = 4
CHUNK = 512


def fused_kernel(
    q_ref, kv_ref, w_ref, res_ref, bl_ref, len_ref, out_ref,
    w_v, kvb, kc, vc, ids_v, ids_s, attb, stg, rl, rr, facc,
    w_sem, ids_sem, kvl_sem, kv_send, kv_recv, at_send, at_recv, z_send, zl_recv, zr_recv,
):
    rows, width = q_ref.shape
    stores, kv_heads, blk, pair = kv_ref.shape
    hd = pair // 2
    n_dp, nz = attb.shape[0], stg.shape[0]
    slots = CAP * n_dp
    local_heads = width // hd
    local_kv = len(kvb) // 2
    head_group = local_heads // local_kv
    per = CHUNK // hd
    groups_per_kv = head_group // per
    n_att = width // CHUNK
    n_col = w_v.shape[0]
    d = lax.axis_index("dp")
    z = lax.axis_index("tensor")
    x, c = d // 2, d % 2
    mate = 2 * x + (1 - c)
    across = 2 * (1 - x) + c
    diag = 2 * (1 - x) + (1 - c)

    def w_copy(j):
        cols = pl.ds(pl.multiple_of(j * CHUNK, CHUNK), CHUNK)
        return pltpu.make_async_copy(w_ref.at[:, cols], w_v.at[j], w_sem.at[j])

    def kv_src(t):
        return kv_ref.at[:, z * local_kv + t // 2, :, pl.ds((t % 2) * hd, hd)]

    def kv_dst(t, owner):
        return kvb[t].at[pl.ds(owner * stores, stores)]

    def kv_local(t):
        return pltpu.make_async_copy(kv_src(t), kv_dst(t, d), kvl_sem.at[t])

    def kv_remote(kind, t):
        owner = across if kind == 2 else d
        src = kv_dst(t, owner) if kind == 2 else kv_src(t)
        return pltpu.make_async_remote_copy(
            src_ref=src, dst_ref=kv_dst(t, owner),
            send_sem=kv_send.at[kind, t], recv_sem=kv_recv.at[kind, t],
            device_id={"dp": across if kind == 1 else mate}, device_id_type=MESH,
        )

    def att_remote(kind, i):
        owner = across if kind == 2 else d
        cols = pl.ds(pl.multiple_of(i * CHUNK, CHUNK), CHUNK)
        ref = attb.at[owner, :, cols]
        return pltpu.make_async_remote_copy(
            src_ref=ref, dst_ref=ref,
            send_sem=at_send.at[kind, i], recv_sem=at_recv.at[kind, i],
            device_id={"dp": across if kind == 1 else mate}, device_id_type=MESH,
        )

    def z_remote(b, j, right):
        cols = pl.ds(pl.multiple_of(j * CHUNK, CHUNK), CHUNK)
        land, sem = (rl, zl_recv) if right else (rr, zr_recv)
        return pltpu.make_async_remote_copy(
            src_ref=stg.at[b, :, cols], dst_ref=land.at[b, :, cols],
            send_sem=z_send.at[b, j], recv_sem=sem.at[b, j],
            device_id={"tensor": z + 1 if right else z - 1}, device_id_type=MESH,
        )

    for t in range(2 * local_kv):
        kv_local(t).start()
    barrier = pltpu.get_barrier_semaphore()
    pl.semaphore_signal(barrier, inc=1, device_id={"dp": mate}, device_id_type=MESH)
    pl.semaphore_signal(barrier, inc=1, device_id={"dp": across}, device_id_type=MESH)

    @pl.when(z > 0)
    def _():
        pl.semaphore_signal(barrier, inc=1, device_id={"tensor": z - 1}, device_id_type=MESH)

    @pl.when(z < nz - 1)
    def _():
        pl.semaphore_signal(barrier, inc=1, device_id={"tensor": z + 1}, device_id_type=MESH)

    pl.semaphore_wait(
        barrier, 2 + (z > 0).astype(jnp.int32) + (z < nz - 1).astype(jnp.int32)
    )

    for t in range(2 * local_kv):
        kv_remote(1, t).start()
    for t in range(2 * local_kv):
        kv_remote(0, t).start()
    for j in range(n_col):
        w_copy(j).start()

    bl = bl_ref[...]
    list_len = bl.shape[0]
    sub = lax.broadcasted_iota(jnp.int32, (128, rows), 0)
    hit = jnp.zeros((128, rows), jnp.int32)
    for k in range(list_len):
        hit = jnp.maximum(hit, (bl[k : k + 1, :] == sub).astype(jnp.int32))
    named_s = jnp.max(hit, axis=1, keepdims=True)
    sub2 = lax.broadcasted_iota(jnp.int32, (128, 128), 0)
    lane2 = lax.broadcasted_iota(jnp.int32, (128, 128), 1)
    named_l = jnp.sum(jnp.where(sub2 == lane2, named_s, 0), axis=0, keepdims=True)
    named_b = jnp.broadcast_to(named_l, (128, 128))
    rank = jnp.sum(jnp.where(lane2 < sub2, named_b, 0), axis=1, keepdims=True)
    picked = jnp.where((rank == lane2) & (named_s > 0), sub2, 0)
    ids = jnp.sum(picked, axis=0, keepdims=True)
    ids_v[...] = jnp.broadcast_to(ids, ids_v.shape)
    ids_copy = pltpu.make_async_copy(ids_v, ids_s, ids_sem)
    ids_copy.start()
    ids_copy.wait()

    place = lax.broadcasted_iota(jnp.int32, (list_len, rows), 0)
    token = lax.broadcasted_iota(jnp.int32, (blk, rows), 0)
    kc[:, hd:] = jnp.zeros((slots * blk, hd), jnp.bfloat16)
    for k in range(slots):
        left = jnp.where(bl == ids_s[0, k], len_ref[...] - place * blk, 0)
        limit = jnp.max(left, axis=0, keepdims=True)
        mask = jnp.where(token < limit, 0.0, -1e30).astype(jnp.bfloat16)
        kc[blk * k : blk * (k + 1), hd : hd + rows] = mask
    vc[:, hd:] = jnp.ones((slots * blk, hd), jnp.bfloat16)
    row_of = lax.broadcasted_iota(jnp.int32, (rows, hd), 0)
    own_row = (row_of == lax.broadcasted_iota(jnp.int32, (rows, hd), 1)).astype(jnp.bfloat16)

    scale = math.log2(math.e) / math.sqrt(hd)
    for h in range(local_kv):
        for t in (2 * h, 2 * h + 1):
            kv_remote(1, t).wait_recv()
            kv_remote(2, t).start()
        for t in (2 * h, 2 * h + 1):
            kv_local(t).wait()
            kv_remote(0, t).wait_recv()
            kv_remote(2, t).wait_recv()
        for j in range(slots):
            pick = ids_s[0, j]
            kc[blk * j : blk * (j + 1), :hd] = kvb[2 * h][pick]
            vc[blk * j : blk * (j + 1), :hd] = kvb[2 * h + 1][pick]

        @pl.loop(0, groups_per_kv)
        def _(g):
            i = h * groups_per_kv + g
            cols = pl.ds(pl.multiple_of(i * CHUNK, CHUNK), CHUNK)
            qs = q_ref[:, cols]
            stacked = jnp.concatenate(
                [
                    jnp.concatenate([qs[:, hd * k : hd * (k + 1)], own_row], axis=1)
                    for k in range(per)
                ],
                axis=0,
            )
            scores = lax.dot_general(
                stacked, kc[...], (((1,), (1,)), ((), ())), preferred_element_type=jnp.float32
            )
            top = jnp.max(scores, axis=1, keepdims=True)
            weights = jnp.exp2((scores - top) * scale).astype(jnp.bfloat16)
            summed = jnp.dot(weights, vc[...], preferred_element_type=jnp.float32)
            attended = (summed[:, :hd] / summed[:, hd:]).astype(jnp.bfloat16).reshape(per, rows, hd)
            attb[d, :, cols] = jnp.concatenate([attended[k] for k in range(per)], axis=1)
            att_remote(1, i).start()
            att_remote(0, i).start()

    @pl.loop(0, n_att)
    def _(i):
        att_remote(0, i).wait_recv()

    inner = (z > 0) & (z < nz - 1)
    half = nz // 2

    def block_of(s, i):
        chip = jnp.where(s < n_col, x, 1 - x)
        return 2 * chip + jnp.where(z < half, 1 - i, i)

    def send_end(s):
        j = s % n_col
        for i in range(2):
            b = block_of(s, i)

            @pl.when((z == 0) & (b > 0))
            def _():
                z_remote(b, j, True).start()

            @pl.when((z == nz - 1) & (b < nz - 1))
            def _():
                z_remote(b, j, False).start()

    def send_inner(s):
        j = s % n_col
        cols = pl.ds(pl.multiple_of(j * CHUNK, CHUNK), CHUNK)

        def pass_on(b, right):
            land = rl if right else rr
            z_remote(b, j, right).wait_recv()
            added = stg[b, :, cols].astype(jnp.float32) + land[b, :, cols].astype(jnp.float32)
            stg[b, :, cols] = added.astype(jnp.bfloat16)
            z_remote(b, j, right).start()

        for i in range(2):
            b = block_of(s, i)

            @pl.when(inner & (b > z))
            def _():
                pass_on(b, True)

            @pl.when(inner & (b < z))
            def _():
                pass_on(b, False)

    def project(s):
        j = s % n_col
        cols = pl.ds(pl.multiple_of(j * CHUNK, CHUNK), CHUNK)

        @pl.when(s < n_col)
        def _():
            w_copy(j).wait()
            att_remote(1, j).wait_recv()
            att_remote(2, j).start()

        @pl.when(s == n_col)
        def _():
            @pl.loop(0, n_att)
            def _(i):
                att_remote(2, i).wait_recv()

        chip = jnp.where(s < n_col, x, 1 - x)
        part = attb[pl.ds(2 * chip, 2)].reshape(2 * rows, width)
        partial = jnp.dot(part, w_v[j], preferred_element_type=jnp.float32)
        stg[pl.ds(2 * chip, 2), :, cols] = partial.astype(jnp.bfloat16).reshape(2, rows, CHUNK)
        send_end(s)

    lag = n_col // 2

    @pl.loop(0, n_col + lag)
    def _(m):
        @pl.when(m < n_col)
        def _():
            @pl.loop(2 * m, 2 * m + 2)
            def _(s):
                project(s)

            send_inner(m)

        @pl.when(m >= lag)
        def _():
            send_inner(n_col + m - lag)

    @pl.loop(0, n_col)
    def _(j):
        cols = pl.ds(pl.multiple_of(j * CHUNK, CHUNK), CHUNK)
        facc[...] = res_ref[:, cols].astype(jnp.float32) + stg[z, :, cols].astype(jnp.float32)

        @pl.when(z > 0)
        def _():
            z_remote(z, j, True).wait_recv()
            facc[...] += rl[z, :, cols].astype(jnp.float32)

        @pl.when(z < nz - 1)
        def _():
            z_remote(z, j, False).wait_recv()
            facc[...] += rr[z, :, cols].astype(jnp.float32)

        out_ref[:, cols] = facc[...].astype(jnp.bfloat16)

    for kind in range(3):
        for t in range(2 * local_kv):
            kv_remote(kind, t).wait_send()

        @pl.loop(0, n_att)
        def _(i):
            att_remote(kind, i).wait_send()

    @pl.loop(0, n_col)
    def _(j):
        for b in range(nz):

            @pl.when(z < b)
            def _():
                z_remote(b, j, True).wait_send()

            @pl.when(z > b)
            def _():
                z_remote(b, j, False).wait_send()


def fused_device(queries, kv_pool, out_weight, residual, block_lists, lengths):
    n_dp, nz = lax.axis_size("dp"), lax.axis_size("tensor")
    rows, width = queries.shape
    stores, kv_heads, blk, pair = kv_pool.shape
    hd = pair // 2
    columns = out_weight.shape[1]
    local_kv = kv_heads // nz
    n_att, n_col = width // CHUNK, columns // CHUNK
    tokens = CAP * n_dp * blk
    bf16, f32 = jnp.bfloat16, jnp.float32
    dma = pltpu.SemaphoreType.DMA
    vmem = pl.BlockSpec(memory_space=pltpu.VMEM)
    hbm = pl.BlockSpec(memory_space=pl.ANY)
    return pl.pallas_call(
        fused_kernel,
        out_shape=jax.ShapeDtypeStruct((rows, columns), bf16),
        in_specs=[vmem, hbm, hbm, vmem, vmem, vmem],
        out_specs=vmem,
        scratch_shapes=[
            pltpu.VMEM((n_col, width, CHUNK), bf16),
            [pltpu.VMEM((n_dp * stores, blk, hd), bf16)] * (2 * local_kv),
            pltpu.VMEM((tokens, 2 * hd), bf16),
            pltpu.VMEM((tokens, 2 * hd), bf16),
            pltpu.VMEM((8, 128), jnp.int32),
            pltpu.SMEM((8, 128), jnp.int32),
            pltpu.VMEM((n_dp, rows, width), bf16),
            pltpu.VMEM((nz, rows, columns), bf16),
            pltpu.VMEM((nz, rows, columns), bf16),
            pltpu.VMEM((nz, rows, columns), bf16),
            pltpu.VMEM((rows, CHUNK), f32),
            dma((n_col,)),
            dma,
            dma((2 * local_kv,)),
            dma((3, 2 * local_kv)),
            dma((3, 2 * local_kv)),
            dma((3, n_att)),
            dma((3, n_att)),
            dma((nz, n_col)),
            dma((nz, n_col)),
            dma((nz, n_col)),
        ],
        compiler_params=pltpu.CompilerParams(
            collective_id=0, has_side_effects=True, vmem_limit_bytes=60 * 1024 * 1024
        ),
        cost_estimate=pl.CostEstimate(
            flops=2 * n_dp * rows * width * columns,
            bytes_accessed=2 * width * columns,
            transcendentals=rows * width // hd * tokens,
        ),
    )(queries, kv_pool, out_weight, residual, block_lists.T, lengths.reshape(1, rows))


def fits_fused(mesh):
    return mesh.shape["dp"] == 4 and mesh.shape["tensor"] == 4


def solution(mesh):
    in_specs = (
        P(("groups", "dp"), "tensor"),
        P(("groups", "dp"), None, None, None),
        P("tensor", "dp"),
        P(("groups", "tensor"), "dp"),
        P(("groups", "dp"), None),
        P(("groups", "dp")),
    )
    out_specs = P(("groups", "tensor"), "dp")
    body = fused_device if fits_fused(mesh) else generic_device
    return jax.shard_map(
        body, mesh=mesh, in_specs=in_specs, out_specs=out_specs, check_vma=False
    )
```

```python
import math

import jax
import jax.numpy as jnp
from jax import lax
from jax.experimental import pallas as pl
from jax.experimental.pallas import tpu as pltpu
from jax.sharding import PartitionSpec as P


def attend_blocks(state_in, query_heads, block_ids, block_data, block_lists, lengths, head_dim):
    row_max, row_total, accumulated = state_in
    block_len = block_data.shape[2]
    list_len = block_lists.shape[1]
    matches = block_lists[:, :, None] == block_ids[None, None, :]
    named_any = jnp.any(matches, axis=1)
    position = jnp.sum(
        matches.astype(jnp.int32) * jnp.arange(list_len, dtype=jnp.int32)[None, :, None], axis=1
    )
    offsets = (
        position[:, :, None] * block_len + jnp.arange(block_len, dtype=jnp.int32)[None, None, :]
    )
    visible = named_any[:, :, None] & (offsets < lengths[:, None, None])
    key_part = block_data[..., :head_dim]
    value_part = block_data[..., head_dim:]
    scores = jnp.einsum(
        "rkqd,nkbd->rkqnb", query_heads, key_part, preferred_element_type=jnp.float32
    ) / math.sqrt(head_dim)
    visible_full = visible[:, None, None, :, :]
    piece_max = jnp.max(jnp.where(visible_full, scores, -1e30), axis=(3, 4))
    new_max = jnp.maximum(row_max, piece_max)
    weights = jnp.where(visible_full, jnp.exp(scores - new_max[..., None, None]), 0.0)
    row_total = jnp.sum(weights, axis=(3, 4))
    accumulated = jnp.einsum(
        "rkqnb,nkbd->rkqd",
        weights.astype(jnp.bfloat16),
        value_part,
        preferred_element_type=jnp.float32,
    )
    return (new_max, row_total, accumulated)


def generic_device(queries, kv_pool, out_weight, residual, block_lists, lengths):
    tensor_size = lax.axis_size("tensor")
    row_count, query_width = queries.shape
    store_count, kv_heads, block_len, pair_width = kv_pool.shape
    head_dim = pair_width // 2
    local_heads = query_width // head_dim
    head_group = local_heads * tensor_size // kv_heads
    local_kv = max(1, local_heads // head_group)
    first_kv = lax.axis_index("tensor") * local_heads // head_group
    own_pool = lax.dynamic_slice_in_dim(kv_pool, first_kv, local_kv, 1)
    query_heads = queries.reshape(row_count, local_kv, local_heads // local_kv, head_dim)
    state_shape = (row_count, local_kv, local_heads // local_kv)
    start_state = (
        jnp.full(state_shape, -1e30, jnp.float32),
        jnp.zeros(state_shape, jnp.float32),
        jnp.zeros(state_shape + (head_dim,), jnp.float32),
    )
    shard_blocks = lax.all_gather(own_pool, "dp", axis=0, tiled=True)
    block_ids = jnp.arange(shard_blocks.shape[0], dtype=jnp.int32)
    final_state = attend_blocks(
        start_state, query_heads, block_ids, shard_blocks, block_lists, lengths, head_dim
    )
    row_max, row_total, accumulated = final_state
    attended = (
        (accumulated / row_total[..., None]).astype(jnp.bfloat16).reshape(row_count, query_width)
    )
    partial_value = jnp.dot(
        lax.all_gather(attended, "dp", axis=0, tiled=True),
        out_weight,
        preferred_element_type=jnp.float32,
    )
    summed = lax.psum_scatter(
        partial_value.astype(jnp.bfloat16), "tensor", scatter_dimension=0, tiled=True
    ).astype(jnp.float32)
    return (residual.astype(jnp.float32) + summed).astype(jnp.bfloat16)


MESH = pl.DeviceIdType.MESH
CAP = 4
CHUNK = 512


def fused_kernel(
    q_ref, kv_ref, w_ref, res_ref, bl_ref, len_ref, out_ref,
    w_v, kvb, kc, vc, ids_v, ids_s, attb, stg, rl, rr, facc,
    w_sem, ids_sem, kvl_sem, kv_send, kv_recv, at_send, at_recv, z_send, zl_recv, zr_recv,
):
    rows, width = q_ref.shape
    stores, kv_heads, blk, pair = kv_ref.shape
    hd = pair // 2
    n_dp, nz = attb.shape[0], stg.shape[0]
    slots = CAP * n_dp
    local_heads = width // hd
    local_kv = len(kvb) // 2
    head_group = local_heads // local_kv
    per = CHUNK // hd
    groups_per_kv = head_group // per
    n_att = width // CHUNK
    n_col = w_v.shape[0]
    d = lax.axis_index("dp")
    z = lax.axis_index("tensor")
    x, c = d // 2, d % 2
    mate = 2 * x + (1 - c)
    across = 2 * (1 - x) + c
    diag = 2 * (1 - x) + (1 - c)

    def w_copy(j):
        cols = pl.ds(pl.multiple_of(j * CHUNK, CHUNK), CHUNK)
        return pltpu.make_async_copy(w_ref.at[:, cols], w_v.at[j], w_sem.at[j])

    def kv_src(t):
        return kv_ref.at[:, z * local_kv + t // 2, :, pl.ds((t % 2) * hd, hd)]

    def kv_dst(t, owner):
        return kvb[t].at[pl.ds(owner * stores, stores)]

    def kv_local(t):
        return pltpu.make_async_copy(kv_src(t), kv_dst(t, d), kvl_sem.at[t])

    def kv_remote(kind, t):
        owner = across if kind == 2 else d
        src = kv_dst(t, owner) if kind == 2 else kv_src(t)
        return pltpu.make_async_remote_copy(
            src_ref=src, dst_ref=kv_dst(t, owner),
            send_sem=kv_send.at[kind, t], recv_sem=kv_recv.at[kind, t],
            device_id={"dp": across if kind == 1 else mate}, device_id_type=MESH,
        )

    def att_remote(kind, i):
        owner = across if kind == 2 else d
        cols = pl.ds(pl.multiple_of(i * CHUNK, CHUNK), CHUNK)
        ref = attb.at[owner, :, cols]
        return pltpu.make_async_remote_copy(
            src_ref=ref, dst_ref=ref,
            send_sem=at_send.at[kind, i], recv_sem=at_recv.at[kind, i],
            device_id={"dp": across if kind == 1 else mate}, device_id_type=MESH,
        )

    def z_remote(b, j, right):
        cols = pl.ds(pl.multiple_of(j * CHUNK, CHUNK), CHUNK)
        land, sem = (rl, zl_recv) if right else (rr, zr_recv)
        return pltpu.make_async_remote_copy(
            src_ref=stg.at[b, :, cols], dst_ref=land.at[b, :, cols],
            send_sem=z_send.at[b, j], recv_sem=sem.at[b, j],
            device_id={"tensor": z + 1 if right else z - 1}, device_id_type=MESH,
        )

    for t in range(2 * local_kv):
        kv_local(t).start()
    barrier = pltpu.get_barrier_semaphore()
    pl.semaphore_signal(barrier, inc=1, device_id={"dp": mate}, device_id_type=MESH)
    pl.semaphore_signal(barrier, inc=1, device_id={"dp": across}, device_id_type=MESH)

    @pl.when(z > 0)
    def _():
        pl.semaphore_signal(barrier, inc=1, device_id={"tensor": z - 1}, device_id_type=MESH)

    @pl.when(z < nz - 1)
    def _():
        pl.semaphore_signal(barrier, inc=1, device_id={"tensor": z + 1}, device_id_type=MESH)

    pl.semaphore_wait(
        barrier, 2 + (z > 0).astype(jnp.int32) + (z < nz - 1).astype(jnp.int32)
    )

    for t in range(2):
        kv_remote(1, t).start()
    for t in range(2 * local_kv):
        kv_remote(0, t).start()
    for j in range(n_col):
        w_copy(j).start()

    bl = bl_ref[...]
    list_len = bl.shape[0]
    sub = lax.broadcasted_iota(jnp.int32, (128, rows), 0)
    hit = jnp.zeros((128, rows), jnp.int32)
    for k in range(list_len):
        hit = jnp.maximum(hit, (bl[k : k + 1, :] == sub).astype(jnp.int32))
    named_s = jnp.max(hit, axis=1, keepdims=True)
    sub2 = lax.broadcasted_iota(jnp.int32, (128, 128), 0)
    lane2 = lax.broadcasted_iota(jnp.int32, (128, 128), 1)
    named_l = jnp.sum(jnp.where(sub2 == lane2, named_s, 0), axis=0, keepdims=True)
    named_b = jnp.broadcast_to(named_l, (128, 128))
    rank = jnp.sum(jnp.where(lane2 < sub2, named_b, 0), axis=1, keepdims=True)
    picked = jnp.where((rank == lane2) & (named_s > 0), sub2, 0)
    ids = jnp.sum(picked, axis=0, keepdims=True)
    ids_v[...] = jnp.broadcast_to(ids, ids_v.shape)
    ids_copy = pltpu.make_async_copy(ids_v, ids_s, ids_sem)
    ids_copy.start()
    ids_copy.wait()

    place = lax.broadcasted_iota(jnp.int32, (list_len, rows), 0)
    token = lax.broadcasted_iota(jnp.int32, (blk, rows), 0)
    kc[:, hd:] = jnp.zeros((slots * blk, hd), jnp.bfloat16)
    for k in range(slots):
        left = jnp.where(bl == ids_s[0, k], len_ref[...] - place * blk, 0)
        limit = jnp.max(left, axis=0, keepdims=True)
        mask = jnp.where(token < limit, 0.0, -1e30).astype(jnp.bfloat16)
        kc[blk * k : blk * (k + 1), hd : hd + rows] = mask
    vc[:, hd:] = jnp.ones((slots * blk, hd), jnp.bfloat16)
    row_of = lax.broadcasted_iota(jnp.int32, (rows, hd), 0)
    own_row = (row_of == lax.broadcasted_iota(jnp.int32, (rows, hd), 1)).astype(jnp.bfloat16)

    scale = math.log2(math.e) / math.sqrt(hd)
    for h in range(local_kv):
        for t in (2 * h, 2 * h + 1):
            kv_remote(1, t).wait_send()
            if h + 1 < local_kv:
                kv_remote(1, t + 2).start()
        for t in (2 * h, 2 * h + 1):
            kv_remote(1, t).wait_recv()
            kv_remote(2, t).start()
        if h + 1 == local_kv:
            for i in range(h * groups_per_kv):
                att_remote(1, i).start()
        for t in (2 * h, 2 * h + 1):
            kv_local(t).wait()
            kv_remote(0, t).wait_recv()
            kv_remote(2, t).wait_recv()
        for j in range(slots):
            pick = ids_s[0, j]
            kc[blk * j : blk * (j + 1), :hd] = kvb[2 * h][pick]
            vc[blk * j : blk * (j + 1), :hd] = kvb[2 * h + 1][pick]

        @pl.loop(0, groups_per_kv)
        def _(g):
            i = h * groups_per_kv + g
            cols = pl.ds(pl.multiple_of(i * CHUNK, CHUNK), CHUNK)
            qs = q_ref[:, cols]
            stacked = jnp.concatenate(
                [
                    jnp.concatenate([qs[:, hd * k : hd * (k + 1)], own_row], axis=1)
                    for k in range(per)
                ],
                axis=0,
            )
            scores = lax.dot_general(
                stacked, kc[...], (((1,), (1,)), ((), ())), preferred_element_type=jnp.float32
            )
            top = jnp.max(scores, axis=1, keepdims=True)
            weights = jnp.exp2((scores - top) * scale).astype(jnp.bfloat16)
            summed = jnp.dot(weights, vc[...], preferred_element_type=jnp.float32)
            attended = (summed[:, :hd] / summed[:, hd:]).astype(jnp.bfloat16).reshape(per, rows, hd)
            attb[d, :, cols] = jnp.concatenate([attended[k] for k in range(per)], axis=1)
            if h + 1 == local_kv:
                att_remote(1, i).start()
            att_remote(0, i).start()

    @pl.loop(0, n_att)
    def _(i):
        att_remote(0, i).wait_recv()

    inner = (z > 0) & (z < nz - 1)
    half = nz // 2
    ahead = 2
    spread = n_att // (n_col // 2)

    def block_of(s, i):
        chip = jnp.where(s < n_col, x, 1 - x)
        return 2 * chip + jnp.where(z < half, 1 - i, i)

    def at_end(s, act):
        j = s % n_col
        for i in range(2):
            b = block_of(s, i)

            @pl.when((z == 0) & (b > 0))
            def _():
                act(z_remote(b, j, True))

            @pl.when((z == nz - 1) & (b < nz - 1))
            def _():
                act(z_remote(b, j, False))

    def send_end(s):
        @pl.when(s >= ahead)
        def _():
            at_end(s - ahead, lambda copy: copy.wait_send())

        at_end(s, lambda copy: copy.start())

    def send_inner(s):
        j = s % n_col
        cols = pl.ds(pl.multiple_of(j * CHUNK, CHUNK), CHUNK)

        def pass_on(b, right):
            land = rl if right else rr
            z_remote(b, j, right).wait_recv()
            added = stg[b, :, cols].astype(jnp.float32) + land[b, :, cols].astype(jnp.float32)
            stg[b, :, cols] = added.astype(jnp.bfloat16)
            z_remote(b, j, right).start()

        for i in range(2):
            b = block_of(s, i)

            @pl.when(inner & (b > z))
            def _():
                pass_on(b, True)

            @pl.when(inner & (b < z))
            def _():
                pass_on(b, False)

    def project(s):
        j = s % n_col
        cols = pl.ds(pl.multiple_of(j * CHUNK, CHUNK), CHUNK)

        @pl.when(s < n_col)
        def _():
            w_copy(j).wait()

        @pl.when((s >= n_col // 2) & (s < n_col))
        def _():
            for k in range(spread):
                i = (j - n_col // 2) * spread + k
                att_remote(1, i).wait_recv()
                att_remote(2, i).start()

        @pl.when(s == n_col)
        def _():
            @pl.loop(0, n_att)
            def _(i):
                att_remote(2, i).wait_recv()

        chip = jnp.where(s < n_col, x, 1 - x)
        part = attb[pl.ds(2 * chip, 2)].reshape(2 * rows, width)
        partial = jnp.dot(part, w_v[j], preferred_element_type=jnp.float32)
        stg[pl.ds(2 * chip, 2), :, cols] = partial.astype(jnp.bfloat16).reshape(2, rows, CHUNK)
        send_end(s)

    lag = n_col // 2

    @pl.loop(0, n_col + lag)
    def _(m):
        @pl.when(m < n_col)
        def _():
            @pl.loop(2 * m, 2 * m + 2)
            def _(s):
                project(s)

            send_inner(m)

        @pl.when(m >= lag)
        def _():
            send_inner(n_col + m - lag)

    @pl.loop(0, n_col)
    def _(j):
        cols = pl.ds(pl.multiple_of(j * CHUNK, CHUNK), CHUNK)
        facc[...] = res_ref[:, cols].astype(jnp.float32) + stg[z, :, cols].astype(jnp.float32)

        @pl.when(z > 0)
        def _():
            z_remote(z, j, True).wait_recv()
            facc[...] += rl[z, :, cols].astype(jnp.float32)

        @pl.when(z < nz - 1)
        def _():
            z_remote(z, j, False).wait_recv()
            facc[...] += rr[z, :, cols].astype(jnp.float32)

        out_ref[:, cols] = facc[...].astype(jnp.bfloat16)

    for kind in range(3):
        if kind != 1:
            for t in range(2 * local_kv):
                kv_remote(kind, t).wait_send()

        @pl.loop(0, n_att)
        def _(i):
            att_remote(kind, i).wait_send()

    for s in range(2 * n_col - ahead, 2 * n_col):
        at_end(s, lambda copy: copy.wait_send())

    @pl.loop(0, n_col)
    def _(j):
        for b in range(nz):

            @pl.when(inner & (z < b))
            def _():
                z_remote(b, j, True).wait_send()

            @pl.when(inner & (z > b))
            def _():
                z_remote(b, j, False).wait_send()


def fused_device(queries, kv_pool, out_weight, residual, block_lists, lengths):
    n_dp, nz = lax.axis_size("dp"), lax.axis_size("tensor")
    rows, width = queries.shape
    stores, kv_heads, blk, pair = kv_pool.shape
    hd = pair // 2
    columns = out_weight.shape[1]
    local_kv = kv_heads // nz
    n_att, n_col = width // CHUNK, columns // CHUNK
    tokens = CAP * n_dp * blk
    bf16, f32 = jnp.bfloat16, jnp.float32
    dma = pltpu.SemaphoreType.DMA
    vmem = pl.BlockSpec(memory_space=pltpu.VMEM)
    hbm = pl.BlockSpec(memory_space=pl.ANY)
    return pl.pallas_call(
        fused_kernel,
        out_shape=jax.ShapeDtypeStruct((rows, columns), bf16),
        in_specs=[vmem, hbm, hbm, vmem, vmem, vmem],
        out_specs=vmem,
        scratch_shapes=[
            pltpu.VMEM((n_col, width, CHUNK), bf16),
            [pltpu.VMEM((n_dp * stores, blk, hd), bf16)] * (2 * local_kv),
            pltpu.VMEM((tokens, 2 * hd), bf16),
            pltpu.VMEM((tokens, 2 * hd), bf16),
            pltpu.VMEM((8, 128), jnp.int32),
            pltpu.SMEM((8, 128), jnp.int32),
            pltpu.VMEM((n_dp, rows, width), bf16),
            pltpu.VMEM((nz, rows, columns), bf16),
            pltpu.VMEM((nz, rows, columns), bf16),
            pltpu.VMEM((nz, rows, columns), bf16),
            pltpu.VMEM((rows, CHUNK), f32),
            dma((n_col,)),
            dma,
            dma((2 * local_kv,)),
            dma((3, 2 * local_kv)),
            dma((3, 2 * local_kv)),
            dma((3, n_att)),
            dma((3, n_att)),
            dma((nz, n_col)),
            dma((nz, n_col)),
            dma((nz, n_col)),
        ],
        compiler_params=pltpu.CompilerParams(
            collective_id=0, has_side_effects=True, vmem_limit_bytes=60 * 1024 * 1024
        ),
        cost_estimate=pl.CostEstimate(
            flops=2 * n_dp * rows * width * columns,
            bytes_accessed=2 * width * columns,
            transcendentals=rows * width // hd * tokens,
        ),
    )(queries, kv_pool, out_weight, residual, block_lists.T, lengths.reshape(1, rows))


def fits_fused(mesh):
    return mesh.shape["dp"] == 4 and mesh.shape["tensor"] == 4


def solution(mesh):
    in_specs = (
        P(("groups", "dp"), "tensor"),
        P(("groups", "dp"), None, None, None),
        P("tensor", "dp"),
        P(("groups", "tensor"), "dp"),
        P(("groups", "dp"), None),
        P(("groups", "dp")),
    )
    out_specs = P(("groups", "tensor"), "dp")
    body = fused_device if fits_fused(mesh) else generic_device
    return jax.shard_map(
        body, mesh=mesh, in_specs=in_specs, out_specs=out_specs, check_vma=False
    )
```

```python
import math

import jax
import jax.numpy as jnp
from jax import lax
from jax.experimental import pallas as pl
from jax.experimental.pallas import tpu as pltpu
from jax.sharding import PartitionSpec as P


def attend_blocks(state_in, query_heads, block_ids, block_data, block_lists, lengths, head_dim):
    row_max, row_total, accumulated = state_in
    block_len = block_data.shape[2]
    list_len = block_lists.shape[1]
    matches = block_lists[:, :, None] == block_ids[None, None, :]
    named_any = jnp.any(matches, axis=1)
    position = jnp.sum(
        matches.astype(jnp.int32) * jnp.arange(list_len, dtype=jnp.int32)[None, :, None], axis=1
    )
    offsets = (
        position[:, :, None] * block_len + jnp.arange(block_len, dtype=jnp.int32)[None, None, :]
    )
    visible = named_any[:, :, None] & (offsets < lengths[:, None, None])
    key_part = block_data[..., :head_dim]
    value_part = block_data[..., head_dim:]
    scores = jnp.einsum(
        "rkqd,nkbd->rkqnb", query_heads, key_part, preferred_element_type=jnp.float32
    ) / math.sqrt(head_dim)
    visible_full = visible[:, None, None, :, :]
    piece_max = jnp.max(jnp.where(visible_full, scores, -1e30), axis=(3, 4))
    new_max = jnp.maximum(row_max, piece_max)
    weights = jnp.where(visible_full, jnp.exp(scores - new_max[..., None, None]), 0.0)
    row_total = jnp.sum(weights, axis=(3, 4))
    accumulated = jnp.einsum(
        "rkqnb,nkbd->rkqd",
        weights.astype(jnp.bfloat16),
        value_part,
        preferred_element_type=jnp.float32,
    )
    return (new_max, row_total, accumulated)


def generic_device(queries, kv_pool, out_weight, residual, block_lists, lengths):
    tensor_size = lax.axis_size("tensor")
    row_count, query_width = queries.shape
    store_count, kv_heads, block_len, pair_width = kv_pool.shape
    head_dim = pair_width // 2
    local_heads = query_width // head_dim
    head_group = local_heads * tensor_size // kv_heads
    local_kv = max(1, local_heads // head_group)
    first_kv = lax.axis_index("tensor") * local_heads // head_group
    own_pool = lax.dynamic_slice_in_dim(kv_pool, first_kv, local_kv, 1)
    query_heads = queries.reshape(row_count, local_kv, local_heads // local_kv, head_dim)
    state_shape = (row_count, local_kv, local_heads // local_kv)
    start_state = (
        jnp.full(state_shape, -1e30, jnp.float32),
        jnp.zeros(state_shape, jnp.float32),
        jnp.zeros(state_shape + (head_dim,), jnp.float32),
    )
    shard_blocks = lax.all_gather(own_pool, "dp", axis=0, tiled=True)
    block_ids = jnp.arange(shard_blocks.shape[0], dtype=jnp.int32)
    final_state = attend_blocks(
        start_state, query_heads, block_ids, shard_blocks, block_lists, lengths, head_dim
    )
    row_max, row_total, accumulated = final_state
    attended = (
        (accumulated / row_total[..., None]).astype(jnp.bfloat16).reshape(row_count, query_width)
    )
    partial_value = jnp.dot(
        lax.all_gather(attended, "dp", axis=0, tiled=True),
        out_weight,
        preferred_element_type=jnp.float32,
    )
    summed = lax.psum_scatter(
        partial_value.astype(jnp.bfloat16), "tensor", scatter_dimension=0, tiled=True
    ).astype(jnp.float32)
    return (residual.astype(jnp.float32) + summed).astype(jnp.bfloat16)


MESH = pl.DeviceIdType.MESH
CAP = 4
CHUNK = 512


def fused_kernel(
    q_ref, kv_ref, w_ref, res_ref, bl_ref, len_ref, out_ref,
    w_v, kvb, kc, vc, ids_v, ids_s, attb, stg, rl, rr, facc,
    w_sem, ids_sem, kvl_sem, kv_send, kv_recv, at_send, at_recv, z_send, zl_recv, zr_recv,
):
    rows, width = q_ref.shape
    stores, kv_heads, blk, pair = kv_ref.shape
    hd = pair // 2
    n_dp, nz = attb.shape[0], stg.shape[0]
    slots = CAP * n_dp
    local_heads = width // hd
    local_kv = len(kvb) // 2
    head_group = local_heads // local_kv
    per = CHUNK // hd
    groups_per_kv = head_group // per
    n_att = width // CHUNK
    n_col = w_v.shape[0]
    d = lax.axis_index("dp")
    z = lax.axis_index("tensor")
    x, c = d // 2, d % 2
    mate = 2 * x + (1 - c)
    across = 2 * (1 - x) + c
    diag = 2 * (1 - x) + (1 - c)

    def w_copy(j):
        cols = pl.ds(pl.multiple_of(j * CHUNK, CHUNK), CHUNK)
        return pltpu.make_async_copy(w_ref.at[:, cols], w_v.at[j], w_sem.at[j])

    def kv_src(t):
        return kv_ref.at[:, z * local_kv + t // 2, :, pl.ds((t % 2) * hd, hd)]

    def kv_dst(t, owner):
        return kvb[t].at[pl.ds(owner * stores, stores)]

    def kv_local(t):
        return pltpu.make_async_copy(kv_src(t), kv_dst(t, d), kvl_sem.at[t])

    def kv_remote(kind, t):
        owner = across if kind == 2 else d
        src = kv_dst(t, owner) if kind == 2 else kv_src(t)
        return pltpu.make_async_remote_copy(
            src_ref=src, dst_ref=kv_dst(t, owner),
            send_sem=kv_send.at[kind, t], recv_sem=kv_recv.at[kind, t],
            device_id={"dp": across if kind == 1 else mate}, device_id_type=MESH,
        )

    def att_remote(kind, i):
        owner = across if kind == 2 else d
        cols = pl.ds(pl.multiple_of(i * CHUNK, CHUNK), CHUNK)
        ref = attb.at[owner, :, cols]
        return pltpu.make_async_remote_copy(
            src_ref=ref, dst_ref=ref,
            send_sem=at_send.at[kind, i], recv_sem=at_recv.at[kind, i],
            device_id={"dp": across if kind == 1 else mate}, device_id_type=MESH,
        )

    def z_remote(b, j, right):
        cols = pl.ds(pl.multiple_of(j * CHUNK, CHUNK), CHUNK)
        land, sem = (rl, zl_recv) if right else (rr, zr_recv)
        return pltpu.make_async_remote_copy(
            src_ref=stg.at[b, :, cols], dst_ref=land.at[b, :, cols],
            send_sem=z_send.at[b, j], recv_sem=sem.at[b, j],
            device_id={"tensor": z + 1 if right else z - 1}, device_id_type=MESH,
        )

    for t in range(2 * local_kv):
        kv_local(t).start()
    barrier = pltpu.get_barrier_semaphore()
    pl.semaphore_signal(barrier, inc=1, device_id={"dp": mate}, device_id_type=MESH)
    pl.semaphore_signal(barrier, inc=1, device_id={"dp": across}, device_id_type=MESH)

    @pl.when(z > 0)
    def _():
        pl.semaphore_signal(barrier, inc=1, device_id={"tensor": z - 1}, device_id_type=MESH)

    @pl.when(z < nz - 1)
    def _():
        pl.semaphore_signal(barrier, inc=1, device_id={"tensor": z + 1}, device_id_type=MESH)

    pl.semaphore_wait(
        barrier, 2 + (z > 0).astype(jnp.int32) + (z < nz - 1).astype(jnp.int32)
    )

    for t in range(2):
        kv_remote(1, t).start()
    for t in range(2 * local_kv):
        kv_remote(0, t).start()
    for j in range(n_col):
        w_copy(j).start()

    bl = bl_ref[...]
    list_len = bl.shape[0]
    sub = lax.broadcasted_iota(jnp.int32, (128, rows), 0)
    hit = jnp.zeros((128, rows), jnp.int32)
    for k in range(list_len):
        hit = jnp.maximum(hit, (bl[k : k + 1, :] == sub).astype(jnp.int32))
    named_s = jnp.max(hit, axis=1, keepdims=True)
    sub2 = lax.broadcasted_iota(jnp.int32, (128, 128), 0)
    lane2 = lax.broadcasted_iota(jnp.int32, (128, 128), 1)
    named_l = jnp.sum(jnp.where(sub2 == lane2, named_s, 0), axis=0, keepdims=True)
    named_b = jnp.broadcast_to(named_l, (128, 128))
    rank = jnp.sum(jnp.where(lane2 < sub2, named_b, 0), axis=1, keepdims=True)
    picked = jnp.where((rank == lane2) & (named_s > 0), sub2, 0)
    ids = jnp.sum(picked, axis=0, keepdims=True)
    ids_v[...] = jnp.broadcast_to(ids, ids_v.shape)
    ids_copy = pltpu.make_async_copy(ids_v, ids_s, ids_sem)
    ids_copy.start()
    ids_copy.wait()

    place = lax.broadcasted_iota(jnp.int32, (list_len, rows), 0)
    token = lax.broadcasted_iota(jnp.int32, (blk, rows), 0)
    kc[:, hd:] = jnp.zeros((slots * blk, hd), jnp.bfloat16)
    for k in range(slots):
        left = jnp.where(bl == ids_s[0, k], len_ref[...] - place * blk, 0)
        limit = jnp.max(left, axis=0, keepdims=True)
        mask = jnp.where(token < limit, 0.0, -1e30).astype(jnp.bfloat16)
        kc[blk * k : blk * (k + 1), hd : hd + rows] = mask
    vc[:, hd:] = jnp.ones((slots * blk, hd), jnp.bfloat16)
    row_of = lax.broadcasted_iota(jnp.int32, (rows, hd), 0)
    own_row = (row_of == lax.broadcasted_iota(jnp.int32, (rows, hd), 1)).astype(jnp.bfloat16)

    scale = math.log2(math.e) / math.sqrt(hd)
    for h in range(local_kv):
        for t in (2 * h, 2 * h + 1):
            kv_remote(1, t).wait_send()
            if h + 1 < local_kv:
                kv_remote(1, t + 2).start()
        for t in (2 * h, 2 * h + 1):
            kv_remote(1, t).wait_recv()
            kv_remote(2, t).start()
        if h + 1 == local_kv:
            for i in range(h * groups_per_kv):
                att_remote(1, i).start()
        for t in (2 * h, 2 * h + 1):
            kv_local(t).wait()
            kv_remote(0, t).wait_recv()
            kv_remote(2, t).wait_recv()
        for j in range(slots):
            pick = ids_s[0, j]
            kc[blk * j : blk * (j + 1), :hd] = kvb[2 * h][pick]
            vc[blk * j : blk * (j + 1), :hd] = kvb[2 * h + 1][pick]

        @pl.loop(0, groups_per_kv)
        def _(g):
            i = h * groups_per_kv + g
            cols = pl.ds(pl.multiple_of(i * CHUNK, CHUNK), CHUNK)
            qs = q_ref[:, cols]
            stacked = jnp.concatenate(
                [
                    jnp.concatenate([qs[:, hd * k : hd * (k + 1)], own_row], axis=1)
                    for k in range(per)
                ],
                axis=0,
            )
            scores = lax.dot_general(
                stacked, kc[...], (((1,), (1,)), ((), ())), preferred_element_type=jnp.float32
            )
            top = jnp.max(scores, axis=1, keepdims=True)
            weights = jnp.exp2((scores - top) * scale).astype(jnp.bfloat16)
            summed = jnp.dot(weights, vc[...], preferred_element_type=jnp.float32)
            attended = (summed[:, :hd] / summed[:, hd:]).astype(jnp.bfloat16).reshape(per, rows, hd)
            attb[d, :, cols] = jnp.concatenate([attended[k] for k in range(per)], axis=1)
            if h + 1 == local_kv:
                att_remote(1, i).start()
            att_remote(0, i).start()

    @pl.loop(0, n_att)
    def _(i):
        att_remote(0, i).wait_recv()

    inner = (z > 0) & (z < nz - 1)
    half = nz // 2
    ahead = 2
    spread = n_att // (n_col // 2)

    def block_of(s, i):
        chip = jnp.where(s < n_col, x, 1 - x)
        return 2 * chip + jnp.where(z < half, 1 - i, i)

    def at_end(s, act):
        j = s % n_col
        for i in range(2):
            b = block_of(s, i)

            @pl.when((z == 0) & (b > 0))
            def _():
                act(z_remote(b, j, True))

            @pl.when((z == nz - 1) & (b < nz - 1))
            def _():
                act(z_remote(b, j, False))

    def send_end(s):
        @pl.when(s >= ahead)
        def _():
            at_end(s - ahead, lambda copy: copy.wait_send())

        at_end(s, lambda copy: copy.start())

    skew = 2

    def send_inner(first, m):
        for right in (True, False):
            j = m - skew * (z - 1 if right else nz - 2 - z)
            cols = pl.ds(pl.multiple_of(j * CHUNK, CHUNK), CHUNK)
            land = rl if right else rr
            for i in range(2):
                b = block_of(first, i)

                @pl.when(inner & (j >= 0) & (j < n_col) & (b > z if right else b < z))
                def _():
                    z_remote(b, j, right).wait_recv()
                    own = stg[b, :, cols].astype(jnp.float32)
                    added = own + land[b, :, cols].astype(jnp.float32)
                    stg[b, :, cols] = added.astype(jnp.bfloat16)
                    z_remote(b, j, right).start()

    def project(s):
        j = s % n_col
        cols = pl.ds(pl.multiple_of(j * CHUNK, CHUNK), CHUNK)

        @pl.when(s < n_col)
        def _():
            w_copy(j).wait()

        @pl.when((s >= n_col // 2) & (s < n_col))
        def _():
            for k in range(spread):
                i = (j - n_col // 2) * spread + k
                att_remote(1, i).wait_recv()
                att_remote(2, i).start()

        @pl.when(s == n_col)
        def _():
            @pl.loop(0, n_att)
            def _(i):
                att_remote(2, i).wait_recv()

        chip = jnp.where(s < n_col, x, 1 - x)
        part = attb[pl.ds(2 * chip, 2)].reshape(2 * rows, width)
        partial = jnp.dot(part, w_v[j], preferred_element_type=jnp.float32)
        stg[pl.ds(2 * chip, 2), :, cols] = partial.astype(jnp.bfloat16).reshape(2, rows, CHUNK)
        send_end(s)

    lag = n_col // 2

    @pl.loop(0, n_col + lag + skew * (nz - 3))
    def _(m):
        @pl.when(m < n_col)
        def _():
            @pl.loop(2 * m, 2 * m + 2)
            def _(s):
                project(s)

        send_inner(0, m)
        send_inner(n_col, m - lag)

    @pl.loop(0, n_col)
    def _(j):
        cols = pl.ds(pl.multiple_of(j * CHUNK, CHUNK), CHUNK)
        facc[...] = res_ref[:, cols].astype(jnp.float32) + stg[z, :, cols].astype(jnp.float32)

        @pl.when(z > 0)
        def _():
            z_remote(z, j, True).wait_recv()
            facc[...] += rl[z, :, cols].astype(jnp.float32)

        @pl.when(z < nz - 1)
        def _():
            z_remote(z, j, False).wait_recv()
            facc[...] += rr[z, :, cols].astype(jnp.float32)

        out_ref[:, cols] = facc[...].astype(jnp.bfloat16)

    for kind in range(3):
        if kind != 1:
            for t in range(2 * local_kv):
                kv_remote(kind, t).wait_send()

        @pl.loop(0, n_att)
        def _(i):
            att_remote(kind, i).wait_send()

    for s in range(2 * n_col - ahead, 2 * n_col):
        at_end(s, lambda copy: copy.wait_send())

    @pl.loop(0, n_col)
    def _(j):
        for b in range(nz):

            @pl.when(inner & (z < b))
            def _():
                z_remote(b, j, True).wait_send()

            @pl.when(inner & (z > b))
            def _():
                z_remote(b, j, False).wait_send()


def fused_device(queries, kv_pool, out_weight, residual, block_lists, lengths):
    n_dp, nz = lax.axis_size("dp"), lax.axis_size("tensor")
    rows, width = queries.shape
    stores, kv_heads, blk, pair = kv_pool.shape
    hd = pair // 2
    columns = out_weight.shape[1]
    local_kv = kv_heads // nz
    n_att, n_col = width // CHUNK, columns // CHUNK
    tokens = CAP * n_dp * blk
    bf16, f32 = jnp.bfloat16, jnp.float32
    dma = pltpu.SemaphoreType.DMA
    vmem = pl.BlockSpec(memory_space=pltpu.VMEM)
    hbm = pl.BlockSpec(memory_space=pl.ANY)
    return pl.pallas_call(
        fused_kernel,
        out_shape=jax.ShapeDtypeStruct((rows, columns), bf16),
        in_specs=[vmem, hbm, hbm, vmem, vmem, vmem],
        out_specs=vmem,
        scratch_shapes=[
            pltpu.VMEM((n_col, width, CHUNK), bf16),
            [pltpu.VMEM((n_dp * stores, blk, hd), bf16)] * (2 * local_kv),
            pltpu.VMEM((tokens, 2 * hd), bf16),
            pltpu.VMEM((tokens, 2 * hd), bf16),
            pltpu.VMEM((8, 128), jnp.int32),
            pltpu.SMEM((8, 128), jnp.int32),
            pltpu.VMEM((n_dp, rows, width), bf16),
            pltpu.VMEM((nz, rows, columns), bf16),
            pltpu.VMEM((nz, rows, columns), bf16),
            pltpu.VMEM((nz, rows, columns), bf16),
            pltpu.VMEM((rows, CHUNK), f32),
            dma((n_col,)),
            dma,
            dma((2 * local_kv,)),
            dma((3, 2 * local_kv)),
            dma((3, 2 * local_kv)),
            dma((3, n_att)),
            dma((3, n_att)),
            dma((nz, n_col)),
            dma((nz, n_col)),
            dma((nz, n_col)),
        ],
        compiler_params=pltpu.CompilerParams(
            collective_id=0, has_side_effects=True, vmem_limit_bytes=60 * 1024 * 1024
        ),
        cost_estimate=pl.CostEstimate(
            flops=2 * n_dp * rows * width * columns,
            bytes_accessed=2 * width * columns,
            transcendentals=rows * width // hd * tokens,
        ),
    )(queries, kv_pool, out_weight, residual, block_lists.T, lengths.reshape(1, rows))


def fits_fused(mesh):
    return mesh.shape["dp"] == 4 and mesh.shape["tensor"] == 4


def solution(mesh):
    in_specs = (
        P(("groups", "dp"), "tensor"),
        P(("groups", "dp"), None, None, None),
        P("tensor", "dp"),
        P(("groups", "tensor"), "dp"),
        P(("groups", "dp"), None),
        P(("groups", "dp")),
    )
    out_specs = P(("groups", "tensor"), "dp")
    body = fused_device if fits_fused(mesh) else generic_device
    return jax.shard_map(
        body, mesh=mesh, in_specs=in_specs, out_specs=out_specs, check_vma=False
    )
```

```python
import math

import jax
import jax.numpy as jnp
from jax import lax
from jax.experimental import pallas as pl
from jax.experimental.pallas import tpu as pltpu
from jax.sharding import PartitionSpec as P


def attend_blocks(state_in, query_heads, block_ids, block_data, block_lists, lengths, head_dim):
    row_max, row_total, accumulated = state_in
    block_len = block_data.shape[2]
    list_len = block_lists.shape[1]
    matches = block_lists[:, :, None] == block_ids[None, None, :]
    named_any = jnp.any(matches, axis=1)
    position = jnp.sum(
        matches.astype(jnp.int32) * jnp.arange(list_len, dtype=jnp.int32)[None, :, None], axis=1
    )
    offsets = (
        position[:, :, None] * block_len + jnp.arange(block_len, dtype=jnp.int32)[None, None, :]
    )
    visible = named_any[:, :, None] & (offsets < lengths[:, None, None])
    key_part = block_data[..., :head_dim]
    value_part = block_data[..., head_dim:]
    scores = jnp.einsum(
        "rkqd,nkbd->rkqnb", query_heads, key_part, preferred_element_type=jnp.float32
    ) / math.sqrt(head_dim)
    visible_full = visible[:, None, None, :, :]
    piece_max = jnp.max(jnp.where(visible_full, scores, -1e30), axis=(3, 4))
    new_max = jnp.maximum(row_max, piece_max)
    weights = jnp.where(visible_full, jnp.exp(scores - new_max[..., None, None]), 0.0)
    row_total = jnp.sum(weights, axis=(3, 4))
    accumulated = jnp.einsum(
        "rkqnb,nkbd->rkqd",
        weights.astype(jnp.bfloat16),
        value_part,
        preferred_element_type=jnp.float32,
    )
    return (new_max, row_total, accumulated)


def generic_device(queries, kv_pool, out_weight, residual, block_lists, lengths):
    tensor_size = lax.axis_size("tensor")
    row_count, query_width = queries.shape
    store_count, kv_heads, block_len, pair_width = kv_pool.shape
    head_dim = pair_width // 2
    local_heads = query_width // head_dim
    head_group = local_heads * tensor_size // kv_heads
    local_kv = max(1, local_heads // head_group)
    first_kv = lax.axis_index("tensor") * local_heads // head_group
    own_pool = lax.dynamic_slice_in_dim(kv_pool, first_kv, local_kv, 1)
    query_heads = queries.reshape(row_count, local_kv, local_heads // local_kv, head_dim)
    state_shape = (row_count, local_kv, local_heads // local_kv)
    start_state = (
        jnp.full(state_shape, -1e30, jnp.float32),
        jnp.zeros(state_shape, jnp.float32),
        jnp.zeros(state_shape + (head_dim,), jnp.float32),
    )
    shard_blocks = lax.all_gather(own_pool, "dp", axis=0, tiled=True)
    block_ids = jnp.arange(shard_blocks.shape[0], dtype=jnp.int32)
    final_state = attend_blocks(
        start_state, query_heads, block_ids, shard_blocks, block_lists, lengths, head_dim
    )
    row_max, row_total, accumulated = final_state
    attended = (
        (accumulated / row_total[..., None]).astype(jnp.bfloat16).reshape(row_count, query_width)
    )
    partial_value = jnp.dot(
        lax.all_gather(attended, "dp", axis=0, tiled=True),
        out_weight,
        preferred_element_type=jnp.float32,
    )
    summed = lax.psum_scatter(
        partial_value.astype(jnp.bfloat16), "tensor", scatter_dimension=0, tiled=True
    ).astype(jnp.float32)
    return (residual.astype(jnp.float32) + summed).astype(jnp.bfloat16)


MESH = pl.DeviceIdType.MESH
CAP = 4
CHUNK = 512


def fused_kernel(
    q_ref, kv_ref, w_ref, res_ref, bl_ref, len_ref, out_ref,
    w_v, kvb, kc, vc, ids_v, ids_s, attb, stg, rl, rr, facc,
    w_sem, ids_sem, kvl_sem, kv_send, kv_recv, at_send, at_recv, z_send, zl_recv, zr_recv,
):
    rows, width = q_ref.shape
    stores, kv_heads, blk, pair = kv_ref.shape
    hd = pair // 2
    n_dp, nz = attb.shape[0], stg.shape[0]
    slots = CAP * n_dp
    local_heads = width // hd
    local_kv = len(kvb) // 2
    head_group = local_heads // local_kv
    per = CHUNK // hd
    groups_per_kv = head_group // per
    n_att = width // CHUNK
    n_col = w_v.shape[0]
    d = lax.axis_index("dp")
    z = lax.axis_index("tensor")
    x, c = d // 2, d % 2
    mate = 2 * x + (1 - c)
    across = 2 * (1 - x) + c
    diag = 2 * (1 - x) + (1 - c)

    def w_copy(j):
        cols = pl.ds(pl.multiple_of(j * CHUNK, CHUNK), CHUNK)
        return pltpu.make_async_copy(w_ref.at[:, cols], w_v.at[j], w_sem.at[j])

    def kv_src(t):
        return kv_ref.at[:, z * local_kv + t // 2, :, pl.ds((t % 2) * hd, hd)]

    def kv_dst(t, owner):
        return kvb[t].at[pl.ds(owner * stores, stores)]

    def kv_local(t):
        return pltpu.make_async_copy(kv_src(t), kv_dst(t, d), kvl_sem.at[t])

    def kv_remote(kind, t):
        owner = across if kind == 2 else d
        src = kv_dst(t, owner) if kind == 2 else kv_src(t)
        return pltpu.make_async_remote_copy(
            src_ref=src, dst_ref=kv_dst(t, owner),
            send_sem=kv_send.at[kind, t], recv_sem=kv_recv.at[kind, t],
            device_id={"dp": across if kind == 1 else mate}, device_id_type=MESH,
        )

    def att_remote(kind, i):
        owner = across if kind == 2 else d
        cols = pl.ds(pl.multiple_of(i * CHUNK, CHUNK), CHUNK)
        ref = attb.at[owner, :, cols]
        return pltpu.make_async_remote_copy(
            src_ref=ref, dst_ref=ref,
            send_sem=at_send.at[kind, i], recv_sem=at_recv.at[kind, i],
            device_id={"dp": across if kind == 1 else mate}, device_id_type=MESH,
        )

    def z_remote(b, j, right):
        cols = pl.ds(pl.multiple_of(j * CHUNK, CHUNK), CHUNK)
        land, sem = (rl, zl_recv) if right else (rr, zr_recv)
        return pltpu.make_async_remote_copy(
            src_ref=stg.at[b, :, cols], dst_ref=land.at[b, :, cols],
            send_sem=z_send.at[b, j], recv_sem=sem.at[b, j],
            device_id={"tensor": z + 1 if right else z - 1}, device_id_type=MESH,
        )

    for t in range(2 * local_kv):
        kv_local(t).start()
    barrier = pltpu.get_barrier_semaphore()
    pl.semaphore_signal(barrier, inc=1, device_id={"dp": mate}, device_id_type=MESH)
    pl.semaphore_signal(barrier, inc=1, device_id={"dp": across}, device_id_type=MESH)

    @pl.when(z > 0)
    def _():
        pl.semaphore_signal(barrier, inc=1, device_id={"tensor": z - 1}, device_id_type=MESH)

    @pl.when(z < nz - 1)
    def _():
        pl.semaphore_signal(barrier, inc=1, device_id={"tensor": z + 1}, device_id_type=MESH)

    pl.semaphore_wait(
        barrier, 2 + (z > 0).astype(jnp.int32) + (z < nz - 1).astype(jnp.int32)
    )

    for t in range(2):
        kv_remote(1, t).start()
    for t in range(2 * local_kv):
        kv_remote(0, t).start()
    for j in range(n_col):
        w_copy(j).start()

    bl = bl_ref[...]
    list_len = bl.shape[0]
    sub = lax.broadcasted_iota(jnp.int32, (128, rows), 0)
    hit = jnp.zeros((128, rows), jnp.int32)
    for k in range(list_len):
        hit = jnp.maximum(hit, (bl[k : k + 1, :] == sub).astype(jnp.int32))
    named_s = jnp.max(hit, axis=1, keepdims=True)
    sub2 = lax.broadcasted_iota(jnp.int32, (128, 128), 0)
    lane2 = lax.broadcasted_iota(jnp.int32, (128, 128), 1)
    named_l = jnp.sum(jnp.where(sub2 == lane2, named_s, 0), axis=0, keepdims=True)
    named_b = jnp.broadcast_to(named_l, (128, 128))
    rank = jnp.sum(jnp.where(lane2 < sub2, named_b, 0), axis=1, keepdims=True)
    picked = jnp.where((rank == lane2) & (named_s > 0), sub2, 0)
    ids = jnp.sum(picked, axis=0, keepdims=True)
    ids_v[...] = jnp.broadcast_to(ids, ids_v.shape)
    ids_copy = pltpu.make_async_copy(ids_v, ids_s, ids_sem)
    ids_copy.start()
    ids_copy.wait()

    place = lax.broadcasted_iota(jnp.int32, (list_len, rows), 0)
    token = lax.broadcasted_iota(jnp.int32, (blk, rows), 0)
    kc[:, hd:] = jnp.zeros((slots * blk, hd), jnp.bfloat16)
    for k in range(slots):
        left = jnp.where(bl == ids_s[0, k], len_ref[...] - place * blk, 0)
        limit = jnp.max(left, axis=0, keepdims=True)
        mask = jnp.where(token < limit, 0.0, -1e30).astype(jnp.bfloat16)
        kc[blk * k : blk * (k + 1), hd : hd + rows] = mask
    vc[:, hd:] = jnp.ones((slots * blk, hd), jnp.bfloat16)
    row_of = lax.broadcasted_iota(jnp.int32, (rows, hd), 0)
    own_row = (row_of == lax.broadcasted_iota(jnp.int32, (rows, hd), 1)).astype(jnp.bfloat16)

    scale = math.log2(math.e) / math.sqrt(hd)
    for h in range(local_kv):
        for t in (2 * h, 2 * h + 1):
            kv_remote(1, t).wait_send()
            if h + 1 < local_kv:
                kv_remote(1, t + 2).start()
        for t in (2 * h, 2 * h + 1):
            kv_remote(1, t).wait_recv()
            kv_remote(2, t).start()
        if h + 1 == local_kv:
            for i in range(h * groups_per_kv):
                att_remote(1, i).start()
        for t in (2 * h, 2 * h + 1):
            kv_local(t).wait()
            kv_remote(0, t).wait_recv()
            kv_remote(2, t).wait_recv()
        for j in range(slots):
            pick = ids_s[0, j]
            kc[blk * j : blk * (j + 1), :hd] = kvb[2 * h][pick]
            vc[blk * j : blk * (j + 1), :hd] = kvb[2 * h + 1][pick]

        @pl.loop(0, groups_per_kv)
        def _(g):
            i = h * groups_per_kv + g
            cols = pl.ds(pl.multiple_of(i * CHUNK, CHUNK), CHUNK)
            qs = q_ref[:, cols]
            stacked = jnp.concatenate(
                [
                    jnp.concatenate([qs[:, hd * k : hd * (k + 1)], own_row], axis=1)
                    for k in range(per)
                ],
                axis=0,
            )
            scores = lax.dot_general(
                stacked, kc[...], (((1,), (1,)), ((), ())), preferred_element_type=jnp.float32
            )
            top = jnp.max(scores, axis=1, keepdims=True)
            weights = jnp.exp2((scores - top) * scale).astype(jnp.bfloat16)
            summed = jnp.dot(weights, vc[...], preferred_element_type=jnp.float32)
            attended = (summed[:, :hd] / summed[:, hd:]).astype(jnp.bfloat16).reshape(per, rows, hd)
            attb[d, :, cols] = jnp.concatenate([attended[k] for k in range(per)], axis=1)
            if h + 1 == local_kv:
                att_remote(1, i).start()
            att_remote(0, i).start()

    @pl.loop(0, n_att)
    def _(i):
        att_remote(0, i).wait_recv()

    inner = (z > 0) & (z < nz - 1)
    half = nz // 2
    ahead = 3
    spread = n_att // (n_col // 2)

    def block_of(s, i):
        chip = jnp.where(s < n_col, x, 1 - x)
        return 2 * chip + jnp.where(z < half, 1 - i, i)

    def at_end(s, act):
        j = s % n_col
        for i in range(2):
            b = block_of(s, i)

            @pl.when((z == 0) & (b > 0))
            def _():
                act(z_remote(b, j, True))

            @pl.when((z == nz - 1) & (b < nz - 1))
            def _():
                act(z_remote(b, j, False))

    def send_end(s):
        @pl.when(s >= ahead)
        def _():
            at_end(s - ahead, lambda copy: copy.wait_send())

        at_end(s, lambda copy: copy.start())

    skew = 3

    def send_inner(first, m):
        for right in (True, False):
            j = m - skew * (z - 1 if right else nz - 2 - z)
            cols = pl.ds(pl.multiple_of(j * CHUNK, CHUNK), CHUNK)
            land = rl if right else rr
            for i in range(2):
                b = block_of(first, i)

                @pl.when(inner & (j >= 0) & (j < n_col) & (b > z if right else b < z))
                def _():
                    z_remote(b, j, right).wait_recv()
                    own = stg[b, :, cols].astype(jnp.float32)
                    added = own + land[b, :, cols].astype(jnp.float32)
                    stg[b, :, cols] = added.astype(jnp.bfloat16)
                    z_remote(b, j, right).start()

    def project(s):
        j = s % n_col
        cols = pl.ds(pl.multiple_of(j * CHUNK, CHUNK), CHUNK)

        @pl.when(s < n_col)
        def _():
            w_copy(j).wait()

        @pl.when((s >= n_col // 2) & (s < n_col))
        def _():
            for k in range(spread):
                i = (j - n_col // 2) * spread + k
                att_remote(1, i).wait_recv()
                att_remote(2, i).start()

        @pl.when(s == n_col)
        def _():
            @pl.loop(0, n_att)
            def _(i):
                att_remote(2, i).wait_recv()

        chip = jnp.where(s < n_col, x, 1 - x)
        part = attb[pl.ds(2 * chip, 2)].reshape(2 * rows, width)
        partial = jnp.dot(part, w_v[j], preferred_element_type=jnp.float32)
        stg[pl.ds(2 * chip, 2), :, cols] = partial.astype(jnp.bfloat16).reshape(2, rows, CHUNK)
        send_end(s)

    lag = n_col // 2

    @pl.loop(0, n_col + lag + skew * (nz - 3))
    def _(m):
        @pl.when(m < n_col)
        def _():
            @pl.loop(2 * m, 2 * m + 2)
            def _(s):
                project(s)

        send_inner(0, m)
        send_inner(n_col, m - lag)

    @pl.loop(0, n_col)
    def _(j):
        cols = pl.ds(pl.multiple_of(j * CHUNK, CHUNK), CHUNK)
        facc[...] = res_ref[:, cols].astype(jnp.float32) + stg[z, :, cols].astype(jnp.float32)

        @pl.when(z > 0)
        def _():
            z_remote(z, j, True).wait_recv()
            facc[...] += rl[z, :, cols].astype(jnp.float32)

        @pl.when(z < nz - 1)
        def _():
            z_remote(z, j, False).wait_recv()
            facc[...] += rr[z, :, cols].astype(jnp.float32)

        out_ref[:, cols] = facc[...].astype(jnp.bfloat16)

    for kind in range(3):
        if kind != 1:
            for t in range(2 * local_kv):
                kv_remote(kind, t).wait_send()

        @pl.loop(0, n_att)
        def _(i):
            att_remote(kind, i).wait_send()

    for s in range(2 * n_col - ahead, 2 * n_col):
        at_end(s, lambda copy: copy.wait_send())

    @pl.loop(0, n_col)
    def _(j):
        for b in range(nz):

            @pl.when(inner & (z < b))
            def _():
                z_remote(b, j, True).wait_send()

            @pl.when(inner & (z > b))
            def _():
                z_remote(b, j, False).wait_send()


def fused_device(queries, kv_pool, out_weight, residual, block_lists, lengths):
    n_dp, nz = lax.axis_size("dp"), lax.axis_size("tensor")
    rows, width = queries.shape
    stores, kv_heads, blk, pair = kv_pool.shape
    hd = pair // 2
    columns = out_weight.shape[1]
    local_kv = kv_heads // nz
    n_att, n_col = width // CHUNK, columns // CHUNK
    tokens = CAP * n_dp * blk
    bf16, f32 = jnp.bfloat16, jnp.float32
    dma = pltpu.SemaphoreType.DMA
    vmem = pl.BlockSpec(memory_space=pltpu.VMEM)
    hbm = pl.BlockSpec(memory_space=pl.ANY)
    return pl.pallas_call(
        fused_kernel,
        out_shape=jax.ShapeDtypeStruct((rows, columns), bf16),
        in_specs=[vmem, hbm, hbm, vmem, vmem, vmem],
        out_specs=vmem,
        scratch_shapes=[
            pltpu.VMEM((n_col, width, CHUNK), bf16),
            [pltpu.VMEM((n_dp * stores, blk, hd), bf16)] * (2 * local_kv),
            pltpu.VMEM((tokens, 2 * hd), bf16),
            pltpu.VMEM((tokens, 2 * hd), bf16),
            pltpu.VMEM((8, 128), jnp.int32),
            pltpu.SMEM((8, 128), jnp.int32),
            pltpu.VMEM((n_dp, rows, width), bf16),
            pltpu.VMEM((nz, rows, columns), bf16),
            pltpu.VMEM((nz, rows, columns), bf16),
            pltpu.VMEM((nz, rows, columns), bf16),
            pltpu.VMEM((rows, CHUNK), f32),
            dma((n_col,)),
            dma,
            dma((2 * local_kv,)),
            dma((3, 2 * local_kv)),
            dma((3, 2 * local_kv)),
            dma((3, n_att)),
            dma((3, n_att)),
            dma((nz, n_col)),
            dma((nz, n_col)),
            dma((nz, n_col)),
        ],
        compiler_params=pltpu.CompilerParams(
            collective_id=0, has_side_effects=True, vmem_limit_bytes=60 * 1024 * 1024
        ),
        cost_estimate=pl.CostEstimate(
            flops=2 * n_dp * rows * width * columns,
            bytes_accessed=2 * width * columns,
            transcendentals=rows * width // hd * tokens,
        ),
    )(queries, kv_pool, out_weight, residual, block_lists.T, lengths.reshape(1, rows))


def fits_fused(mesh):
    return mesh.shape["dp"] == 4 and mesh.shape["tensor"] == 4


def solution(mesh):
    in_specs = (
        P(("groups", "dp"), "tensor"),
        P(("groups", "dp"), None, None, None),
        P("tensor", "dp"),
        P(("groups", "tensor"), "dp"),
        P(("groups", "dp"), None),
        P(("groups", "dp")),
    )
    out_specs = P(("groups", "tensor"), "dp")
    body = fused_device if fits_fused(mesh) else generic_device
    return jax.shard_map(
        body, mesh=mesh, in_specs=in_specs, out_specs=out_specs, check_vma=False
    )
```
